32 devices in a mesh: cells: 4 (over y, x), wall: 8 (over z, core).
Axes of the slice: x: 2, y: 2, z: 4, core: 2. Of those that a mesh axis runs over, the one named last changes fastest.
Arguments:
- shape_coef: bfloat16 [3, 289, 8192], P(None, None, ('cells', 'wall')), may hold values from -3 to 3
- force_coef: bfloat16 [3, 289, 8192], P(None, None, ('cells', 'wall')), may hold values from -1.5 to 1.5
- near_cell: int32 [2048], P(('cells', 'wall')), may hold values from 0 to 255
- near_dest: int32 [2048], P(('cells', 'wall')), may hold values from 0 to 7, as said below
- near_slot: int32 [2048], P(('cells', 'wall')), may hold values from 0 to 1
- panel_centers: float32 [64, 384], P(('cells', 'wall')), may hold values from -2 to 2
- near_blocks: bfloat16 [64, 2, 384, 384], P(('cells', 'wall')), may hold values from -0.15625 to 0.15625
- near_pick: int32 [64], P(('cells', 'wall')), may hold values from 0 to 1
- src_basis: float32 [64, 384, 16], P(('cells', 'wall')), may hold values from -0.3125 to 0.3125
- far_couple: float32 [64, 8, 16, 16], P(('cells', 'wall')), may hold values from -0.5 to 0.5
- far_src: int32 [64, 8], P(('cells', 'wall')), may hold values from 0 to 63
- far_rank: int32 [64, 8], P(('cells', 'wall')), may hold values from 1 to 16
- tgt_basis: float32 [64, 16, 384], P(('cells', 'wall')), may hold values from -1.5 to 1.5
- cluster_slot: int32 [64], replicated, may hold values from 0 to 63, each once
Outputs:
- surface: bfloat16 [3, 578, 8192], P(None, None, ('cells', 'wall'))
- density: float32 [64, 384], P(('cells', 'wall'))
The draws below stay inside these ranges and needn't reach their ends.
Inputs may be any that keep to these rules, and one draw needn't show every extreme that they name: `near_cell`: A cell of the row's own device block of 256 cells; each device holds 64 rows. `near_dest`: among the 64 rows of one device no value appears more than 16 times; in each group of 8 devices along the wall axis some value appears exactly 16 times among the rows of every device of the group. `cluster_slot`: each of 0 to 63 appears once.
All inputs are finite; a program needn't handle non-finite values.
Results may differ from the reference program's by a relative error of at most 0.0062.
Values may be sent and summed in bfloat16 or wider, within the bound.
A program may use at most 64 MiB of HBM per device.

```python
import math
import jax
import jax.numpy as jnp
import numpy as np
from jax import lax

ORDER = 16
SH = 289
C_DEV = 256
CELLS = 8192
NEAR_DEV = 64
NEAR_TOTAL = 2048
CAP = 16
PAN = 128
CL_DEV = 2
NCL = 64
RANK = 16
FB = 8
ITERS = 2
N_WALL = 8


def draw_near_dest(key, part):
    devices_all = NEAR_TOTAL // NEAR_DEV
    groups = devices_all // N_WALL
    hot_dest = jax.random.randint(jax.random.fold_in(key, 11), (groups,), 0, N_WALL)
    hot_device = jnp.repeat(hot_dest, N_WALL)
    keys = jax.random.split(jax.random.fold_in(key, 12), devices_all)

    def device_rows(device_key, hot_one):
        key_items, key_order = jax.random.split(device_key)
        picked_items = jax.random.permutation(key_items, (N_WALL - 1) * CAP)[:NEAR_DEV - CAP]
        other_dest = (picked_items // CAP).astype(jnp.int32)
        other_dest = other_dest + (other_dest >= hot_one).astype(jnp.int32)
        dest_rows = jnp.concatenate([jnp.full((CAP,), hot_one, jnp.int32), other_dest])
        row_order = jax.random.permutation(key_order, NEAR_DEV)
        return dest_rows[row_order]
    return jax.vmap(device_rows)(keys, hot_device).reshape(-1).astype(jnp.int32)


def with_ends(entries, own_key, least, top_value):
    longest = entries.shape.index(max(entries.shape))
    spots = []
    for shift in (0, 1):
        where = [jax.random.randint(jax.random.fold_in(own_key, axis), (), 0, length) for axis, length in enumerate(entries.shape)]
        where[longest] = (where[longest] + shift) % entries.shape[longest]
        spots.append(tuple(where))
    return entries.at[spots[0]].set(least).at[spots[1]].set(top_value)


def steps_of(stream_key, extent, cuts, least, top_value):
    level = 1.0
    for dim, shards_of in cuts:
        draws = jax.random.uniform(jax.random.fold_in(jax.random.fold_in(stream_key, 6), dim), (shards_of,), jnp.float32, least / len(cuts), top_value / len(cuts))
        level = level * jnp.repeat(jnp.exp(draws), extent[dim] // shards_of).reshape((-1,) + (1,) * (len(extent) - 1 - dim))
    return level


def normal_values(own_key, dims, scale, most, cuts=(), kind=jnp.bfloat16):
    values = jax.random.normal(own_key, dims, jnp.float32) * scale
    if len(cuts) > 0:
        values = steps_of(own_key, dims, cuts, -0.22, 0.18) * values
    return jnp.clip(values, min=-most, max=most).astype(kind)


def setup_inputs(seed: int = 0) -> dict:
    key_of = jax.random.split(jax.random.key(seed), 15)
    return {
        "shape_coef": normal_values(key_of[0], (3, SH, CELLS), 0.2, 3.0, ((2, 32),)),
        "force_coef": normal_values(key_of[1], (3, SH, CELLS), 0.1, 1.5, ((2, 32),)),
        "near_cell": with_ends(jax.random.randint(key_of[2], (NEAR_TOTAL,), 0, C_DEV), jax.random.fold_in(key_of[2], 1), 0, C_DEV - 1).astype(jnp.int32),
        "near_dest": draw_near_dest(jax.random.fold_in(key_of[14], 71), 0),
        "near_slot": with_ends(jax.random.randint(key_of[4], (NEAR_TOTAL,), 0, CL_DEV), jax.random.fold_in(key_of[4], 1), 0, CL_DEV - 1).astype(jnp.int32),
        "panel_centers": jnp.clip(jax.random.uniform(key_of[5], (NCL, 3 * PAN), jnp.float32, -2.0, 2.0) * steps_of(key_of[5], (NCL, 3 * PAN), ((0, 32),), -0.4, 0.0), -2.0, 2.0),
        "near_blocks": normal_values(key_of[6], (NCL, 2, 3 * PAN, 3 * PAN), (12 * PAN) ** -0.5, 0.15625, ((0, 32),)),
        "near_pick": with_ends(jax.random.randint(key_of[7], (NCL,), 0, CL_DEV), jax.random.fold_in(key_of[7], 1), 0, CL_DEV - 1).astype(jnp.int32),
        "src_basis": normal_values(key_of[8], (NCL, 3 * PAN, RANK), (3 * PAN) ** -0.5, 0.3125, ((0, 32),), jnp.float32),
        "far_couple": normal_values(key_of[9], (NCL, FB, RANK, RANK), (RANK * FB) ** -0.5, 0.5, ((0, 32),), jnp.float32),
        "far_src": with_ends(jax.random.randint(key_of[10], (NCL, FB), 0, NCL), jax.random.fold_in(key_of[10], 1), 0, NCL - 1).astype(jnp.int32),
        "far_rank": with_ends(jax.random.randint(key_of[11], (NCL, FB), 1, RANK + 1), jax.random.fold_in(key_of[11], 1), 1, RANK).astype(jnp.int32),
        "tgt_basis": normal_values(key_of[12], (NCL, RANK, 3 * PAN), RANK ** -0.5, 1.5, ((0, 32),), jnp.float32),
        "cluster_slot": jax.random.permutation(key_of[13], NCL).astype(jnp.int32),
    }


soft_core = 0.25
stokes_scale = 1.0 / (8.0 * math.pi)

def harmonics(order):
    lat_count = order + 1
    polar_angle = np.pi * (np.arange(lat_count) + 0.5) / lat_count
    azimuth = np.pi * np.arange(2 * lat_count) / lat_count
    cos_polar = np.repeat(np.cos(polar_angle), 2 * lat_count)
    sin_polar = np.repeat(np.sin(polar_angle), 2 * lat_count)
    az_grid = np.tile(azimuth, lat_count)
    legendre = {}
    legendre[0, 0] = cos_polar * 0.0 + 0.5 / np.sqrt(np.pi)
    for m in range(1, order + 1):
        legendre[m, m] = -np.sqrt((2.0 * m + 1.0) / (2.0 * m)) * sin_polar * legendre[m - 1, m - 1]
    for m in range(order):
        legendre[m + 1, m] = np.sqrt(2.0 * m + 3.0) * cos_polar * legendre[m, m]
    for m in range(order + 1):
        for l in range(m + 2, order + 1):
            factor = np.sqrt((4.0 * l * l - 1.0) / (l * l - m * m))
            backward = np.sqrt(((l - 1.0) ** 2 - m * m) / (4.0 * (l - 1.0) ** 2 - 1.0))
            legendre[l, m] = factor * (cos_polar * legendre[l - 1, m] - backward * legendre[l - 2, m])
    columns = []
    for l in range(order + 1):
        for m in range(-l, l + 1):
            if m > 0:
                columns.append(np.sqrt(2.0) * legendre[l, m] * np.cos(m * az_grid))
            elif m < 0:
                columns.append(np.sqrt(2.0) * legendre[l, -m] * np.sin(-m * az_grid))
            else:
                columns.append(legendre[l, 0])
    return np.stack(columns, axis=1)

def kernel_block(pieces):
    points, forces, centers = pieces
    panels = centers.shape[1] // 3
    source = points.astype(jnp.float32)
    strength = forces.astype(jnp.float32)
    spots = centers.reshape(centers.shape[0], 3, panels)
    offset = [spots[:, a, :, None] - source[:, a, None, :] for a in range(3)]
    radius_sq = offset[0] * offset[0] + offset[1] * offset[1] + offset[2] * offset[2] + soft_core
    inverse = lax.rsqrt(radius_sq)
    inverse_cube = inverse * inverse * inverse
    along = offset[0] * strength[:, 0, None, :] + offset[1] * strength[:, 1, None, :] + offset[2] * strength[:, 2, None, :]
    parts = [lax.optimization_barrier(jnp.sum(strength[:, a, None, :] * inverse + offset[a] * along * inverse_cube, axis=2)) for a in range(3)]
    return jnp.stack(parts, axis=1).reshape(centers.shape[0], 3 * panels) * stokes_scale

def stokes_rows(points, forces, centers, block):
    total = points.shape[0]
    width = math.gcd(total, block)
    groups = total // width
    result = lax.map(kernel_block, (points.reshape(groups, width, 3, points.shape[2]), forces.reshape(groups, width, 3, forces.shape[2]), centers.reshape(groups, width, centers.shape[1])))
    return result.reshape(total, centers.shape[1])

def near_apply(pair_args):
    blocks, vectors = pair_args
    return jnp.einsum('bij,bj->i', blocks.astype(jnp.float32), vectors, precision=lax.Precision.HIGHEST)

def reference(shape_coef, force_coef, near_cell, near_dest, near_slot, panel_centers, near_blocks, near_pick, src_basis, far_couple, far_src, far_rank, tgt_basis, cluster_slot):
    harmonic = jnp.asarray(harmonics(ORDER), jnp.float32).astype(jnp.bfloat16)
    harmonic_wide = harmonic.astype(jnp.float32)
    surface = jnp.einsum('qs,asc->aqc', harmonic_wide, shape_coef.astype(jnp.float32), precision=lax.Precision.HIGHEST).astype(jnp.bfloat16)
    row_ids = jnp.arange(NEAR_TOTAL, dtype=jnp.int32)
    source = row_ids // NEAR_DEV
    cell_ids = (source * C_DEV + near_cell).astype(jnp.int32)
    points = jnp.transpose(jnp.take(surface, cell_ids, axis=2), (2, 0, 1))
    picked = jnp.take(force_coef, cell_ids, axis=2).astype(jnp.float32)
    forces = jnp.einsum('qs,asn->naq', harmonic_wide, picked, precision=lax.Precision.HIGHEST).astype(jnp.bfloat16)
    target = ((source // N_WALL * N_WALL + near_dest) * CL_DEV + near_slot).astype(jnp.int32)
    centers = jnp.take(panel_centers, target, axis=0)
    velocity = stokes_rows(points, forces, centers, 64)
    wall_rhs = -jax.ops.segment_sum(velocity, target, num_segments=NCL)
    clusters = jnp.arange(NCL, dtype=jnp.int32)
    owner = clusters // CL_DEV
    previous = owner // N_WALL * N_WALL + (owner % N_WALL + N_WALL - 1) % N_WALL
    neighbor_ids = (previous * CL_DEV + near_pick).astype(jnp.int32)
    source_rows = jnp.take(cluster_slot, far_src, axis=0).astype(jnp.int32)
    levels = jnp.arange(RANK, dtype=jnp.int32)
    rank_keep = (levels[None, None, :, None] < far_rank[:, :, None, None]) & (levels[None, None, None, :] < far_rank[:, :, None, None])
    masked = jnp.where(rank_keep, far_couple, jnp.zeros_like(far_couple))
    density = wall_rhs
    for step in range(ITERS):
        density_low = lax.optimization_barrier(density.astype(jnp.bfloat16)).astype(jnp.float32)
        paired = jnp.stack([density_low, jnp.take(density_low, neighbor_ids, axis=0)], axis=1)
        near_term = lax.map(near_apply, (near_blocks, paired))
        coefficients = jnp.einsum('cpr,cp->cr', src_basis, density, precision=lax.Precision.HIGHEST)
        gathered = jnp.take(coefficients, source_rows, axis=0)
        mixed_rank = jnp.einsum('cbij,cbj->ci', masked, gathered, precision=lax.Precision.HIGHEST)
        far_term = jnp.einsum('cr,crp->cp', mixed_rank, tgt_basis, precision=lax.Precision.HIGHEST)
        density = wall_rhs - near_term - far_term
    return (surface, density)
```

```python
import functools
import math

import jax
import jax.numpy as jnp
import numpy as np
from jax import lax
from jax.experimental import pallas as pl
from jax.experimental.pallas import tpu as pltpu
from jax.sharding import PartitionSpec as P

ORDER = 16
ITERS = 2
LANES = 128
ROWS = 16

soft_core = 0.25
stokes_scale = 1.0 / (8.0 * math.pi)

MESH = pl.DeviceIdType.MESH
HIGHEST = lax.Precision.HIGHEST
F32 = jnp.float32
BF16 = jnp.bfloat16
NT = (((1,), (1,)), ((), ()))


def harmonics(order):
    lat_count = order + 1
    polar_angle = np.pi * (np.arange(lat_count) + 0.5) / lat_count
    azimuth = np.pi * np.arange(2 * lat_count) / lat_count
    cos_polar = np.repeat(np.cos(polar_angle), 2 * lat_count)
    sin_polar = np.repeat(np.sin(polar_angle), 2 * lat_count)
    az_grid = np.tile(azimuth, lat_count)
    legendre = {}
    legendre[0, 0] = cos_polar * 0.0 + 0.5 / np.sqrt(np.pi)
    for m in range(1, order + 1):
        legendre[m, m] = -np.sqrt((2.0 * m + 1.0) / (2.0 * m)) * sin_polar * legendre[m - 1, m - 1]
    for m in range(order):
        legendre[m + 1, m] = np.sqrt(2.0 * m + 3.0) * cos_polar * legendre[m, m]
    for m in range(order + 1):
        for l in range(m + 2, order + 1):
            factor = np.sqrt((4.0 * l * l - 1.0) / (l * l - m * m))
            backward = np.sqrt(((l - 1.0) ** 2 - m * m) / (4.0 * (l - 1.0) ** 2 - 1.0))
            legendre[l, m] = factor * (
                cos_polar * legendre[l - 1, m] - backward * legendre[l - 2, m]
            )
    columns = []
    for l in range(order + 1):
        for m in range(-l, l + 1):
            if m > 0:
                columns.append(np.sqrt(2.0) * legendre[l, m] * np.cos(m * az_grid))
            elif m < 0:
                columns.append(np.sqrt(2.0) * legendre[l, -m] * np.sin(-m * az_grid))
            else:
                columns.append(legendre[l, 0])
    return np.stack(columns, axis=1)


def each(count, body):
    if count <= 16:
        for i in range(count):
            body(i)
    else:
        def step(i, carry):
            body(i)
            return carry

        lax.fori_loop(0, count, step, 0)


def rounded(value):
    return value.astype(BF16).astype(F32)


def split3(value):
    first = rounded(value)
    rest = value - first
    second = rounded(rest)
    return first, second, rounded(rest - second)


def wall_kernel(
    cells,
    walls,
    dest_s,
    slot_s,
    pick_s,
    src_s,
    rank_s,
    owner_s,
    cell_ref,
    dest_ref,
    slot_ref,
    harm_ref,
    shape_ref,
    force_ref,
    centers_ref,
    blocks_ref,
    srcb_ref,
    couple_ref,
    tgtb_ref,
    out_ref,
    b_sc,
    a_sc,
    at_sc,
    x_sc,
    v_sc,
    s_sc,
    part_sc,
    recv_sc,
    stage_sc,
    mask_sc,
    wall_send,
    wall_recv,
    cell_send,
    cell_recv,
    ring_send,
    ring_recv,
    *step_sc,
):
    clusters = centers_ref.shape[0]
    panels = centers_ref.shape[1] // 3
    near = dest_ref.shape[1]
    group = walls * clusters
    chunks = b_sc.shape[2] // (2 * LANES)
    me_cell = lax.axis_index("cells")
    me = lax.axis_index("wall")

    def wall_peer(d):
        return lax.rem(me + d, walls)

    def cell_peer(d):
        return lax.rem(me_cell + d, cells)

    barrier = pltpu.get_barrier_semaphore()

    def greet_wall(i):
        pl.semaphore_signal(barrier, inc=1, device_id={"wall": wall_peer(i + 1)}, device_id_type=MESH)

    def greet_cell(i):
        pl.semaphore_signal(barrier, inc=1, device_id={"cells": cell_peer(i + 1)}, device_id_type=MESH)

    each(walls - 1, greet_wall)
    each(cells - 1, greet_cell)

    for s in range(clusters):
        x_sc[me * clusters + s] = centers_ref[s : s + 1, :]

    def column(row):
        size = row.shape[1]
        down = lax.broadcasted_iota(jnp.int32, (size, size), 0)
        across = lax.broadcasted_iota(jnp.int32, (size, size), 1)
        return jnp.sum(jnp.where(down == across, row, 0.0), axis=1, keepdims=True)

    cell_col = column(cell_ref[...].astype(F32))
    cell_count = shape_ref.shape[2]
    lane_cell = lax.broadcasted_iota(jnp.int32, (near, cell_count), 1).astype(F32)
    onehot = (lane_cell == cell_col).astype(BF16)

    def on_grid(ref, a):
        picked = lax.dot_general(onehot, ref[a], NT, preferred_element_type=F32).astype(BF16)
        return rounded(jnp.dot(picked, harm_ref[...], preferred_element_type=F32))

    def put(row, half, value):
        for j in range(chunks):
            at = (2 * j + half) * LANES
            b_sc[:, row, at : at + LANES] = value[:, j * LANES : (j + 1) * LANES]

    points = [on_grid(shape_ref, a) for a in range(3)]

    pl.semaphore_wait(barrier, walls + cells - 2)

    def wall_copy(phase, d, src, dst):
        return pltpu.make_async_remote_copy(
            src_ref=src,
            dst_ref=dst,
            send_sem=wall_send.at[phase, d],
            recv_sem=wall_recv.at[phase, d],
            device_id={"wall": wall_peer(d)},
            device_id_type=MESH,
        )

    own = pl.ds(me * clusters, clusters)

    def center_copy(d):
        return wall_copy(0, d, x_sc.at[own], x_sc.at[own])

    each(walls - 1, lambda i: center_copy(i + 1).start())

    forces = [on_grid(force_ref, a) for a in range(3)]
    zero = jnp.zeros_like(points[0])
    one = zero + 1.0
    square = points[0] * points[0] + points[1] * points[1] + points[2] * points[2] + soft_core
    inner = points[0] * forces[0] + points[1] * forces[1] + points[2] * forces[2]
    for a in range(3):
        double = points[a] * -2.0
        for half, value in ((0, double), (1, forces[a])):
            put(a, half, value)
            put(3 + a, half, value)
        put(12 + a, 0, points[a])
        put(12 + a, 1, zero)
        put(9 + a, 0, one)
        put(9 + a, 1, zero)
    for a, (sq, inn) in enumerate(zip(split3(square), split3(inner))):
        put(6 + a, 0, sq)
        put(6 + a, 1, -inn)
    put(15, 0, zero)
    put(15, 1, zero)

    rank_size = couple_ref.shape[2]
    far_blocks = couple_ref.shape[1]
    level_i = lax.broadcasted_iota(jnp.int32, (rank_size, rank_size), 0)
    level_j = lax.broadcasted_iota(jnp.int32, (rank_size, rank_size), 1)
    level = jnp.maximum(level_i, level_j)
    for t in range(clusters):
        for b in range(far_blocks):
            mask_sc[t, b] = jnp.where(level < rank_s[t, b], couple_ref[t, b], 0.0)

    each(walls - 1, lambda i: center_copy(i + 1).wait())

    def make_panels(t):
        for a in range(3):
            spot = x_sc[t][:, a * panels : (a + 1) * panels]
            first = rounded(spot)
            second = rounded(spot - first)
            held = first + second
            at_sc[a : a + 1, :] = first
            at_sc[3 + a : 4 + a, :] = second
            norm = held * held if a == 0 else norm + held * held
        for a, value in enumerate(split3(norm)):
            at_sc[9 + a : 10 + a, :] = value
        a_sc[t] = jnp.transpose(at_sc[...]).astype(BF16)

    at_sc[6:9, :] = jnp.ones((3, panels), F32)
    at_sc[12:16, :] = jnp.zeros((4, panels), F32)
    each(group, make_panels)

    def pair_row(r, carry):
        target = dest_s[r] * clusters + slot_s[r]
        panel = a_sc[target]
        total = jnp.zeros((ROWS, panels), F32)
        for j in range(chunks):
            rows = b_sc[r, :, 2 * j * LANES : 2 * (j + 1) * LANES].astype(BF16)
            both = jnp.dot(panel, rows, preferred_element_type=F32)
            inverse = lax.rsqrt(both[:, :LANES])
            along = both[:, LANES:] * (inverse * inverse * inverse)
            pair = jnp.concatenate([along.astype(BF16), inverse.astype(BF16)], axis=1)
            total += lax.dot_general(rows, pair, NT, preferred_element_type=F32)
        v_sc[pl.ds(pl.multiple_of(r * ROWS, ROWS), ROWS), :] = total
        return carry

    lax.fori_loop(0, near, pair_row, 0, unroll=2)

    flat = near * ROWS
    target_row = (dest_ref[...] * clusters + slot_ref[...]).astype(F32)
    spread = (
        lax.shift_right_logical(lax.broadcasted_iota(jnp.int32, (near, flat), 1), 4)
        == lax.broadcasted_iota(jnp.int32, (near, flat), 0)
    ).astype(F32)
    target_flat = jnp.dot(
        jnp.broadcast_to(target_row, (8, near)), spread, precision=HIGHEST, preferred_element_type=F32
    )[0:1]
    down = lax.broadcasted_iota(jnp.int32, (group * 8, flat), 0)
    across = lax.broadcasted_iota(jnp.int32, (group * 8, flat), 1)
    kind = down & 7
    source = across & (ROWS - 1)
    same = lax.shift_right_logical(down, 3).astype(F32) == target_flat
    use = ((kind < 3) & ((source == kind) | (source == kind + 12))) | ((kind == 3) & (source == 9))
    select = (same & use).astype(F32)
    s_sc[...] = jnp.dot(select, v_sc[...], precision=HIGHEST, preferred_element_type=F32).reshape(
        group, 8, panels
    )

    def make_part(t):
        for a in range(3):
            lanes = slice(a * panels, (a + 1) * panels)
            part_sc[t, :, lanes] = -stokes_scale * (
                s_sc[t, a : a + 1, :] + x_sc[t, :, lanes] * s_sc[t, 3:4, :]
            )

    each(group, make_part)

    def part_copy(d):
        return wall_copy(
            1, d, part_sc.at[pl.ds(wall_peer(d) * clusters, clusters)], recv_sc.at[me]
        )

    each(walls - 1, lambda i: part_copy(i + 1).start())
    recv_sc[me] = part_sc[own]
    each(walls - 1, lambda i: part_copy(i + 1).wait())
    total = jnp.sum(recv_sc[...], axis=0)
    rhs = [total[t] for t in range(clusters)]

    flat_i = lax.broadcasted_iota(jnp.int32, (rank_size, LANES), 0)
    flat_j = lax.broadcasted_iota(jnp.int32, (rank_size, LANES), 1)
    diagonal = flat_i == flat_j
    first_row = me_cell * group

    def apply_block(t, b, vector):
        low = jnp.broadcast_to(vector.astype(BF16), (ROWS, vector.shape[1]))
        return lax.dot_general(low, blocks_ref[t, b], NT, preferred_element_type=F32)[0:1]

    density = rhs
    for step in range(ITERS):
        table_sc, nbr_sc = step_sc[2 * step : 2 * step + 2]
        ring = pltpu.make_async_remote_copy(
            src_ref=stage_sc.at[step],
            dst_ref=nbr_sc,
            send_sem=ring_send.at[step],
            recv_sem=ring_recv.at[step],
            device_id={"wall": wall_peer(1)},
            device_id_type=MESH,
        )
        for t in range(clusters):
            coef = jnp.sum(srcb_ref[t] * density[t], axis=1, keepdims=True)
            table_sc[first_row + me * clusters + t] = jnp.sum(
                jnp.where(diagonal, coef, 0.0), axis=0, keepdims=True
            )
            stage_sc[step, t] = density[t]
        mine = table_sc.at[pl.ds(first_row + me * clusters, clusters)]

        def coef_copy(d):
            return wall_copy(2 + step, d, mine, mine)

        each(walls - 1, lambda i: coef_copy(i + 1).start())
        ring.start()
        near_term = [apply_block(t, 0, density[t]) for t in range(clusters)]
        each(walls - 1, lambda i: coef_copy(i + 1).wait())
        block = table_sc.at[pl.ds(first_row, group)]

        def block_copy(d):
            return pltpu.make_async_remote_copy(
                src_ref=block,
                dst_ref=block,
                send_sem=cell_send.at[step, d],
                recv_sem=cell_recv.at[step, d],
                device_id={"cells": cell_peer(d)},
                device_id_type=MESH,
            )

        each(cells - 1, lambda i: block_copy(i + 1).start())
        ring.wait()
        near_term = [
            near_term[t] + apply_block(t, 1, nbr_sc[pick_s[t]]) for t in range(clusters)
        ]
        each(cells - 1, lambda i: block_copy(i + 1).wait())
        fresh = []
        for t in range(clusters):
            mixed = jnp.zeros((rank_size, rank_size), F32)
            for b in range(far_blocks):
                row = table_sc[owner_s[src_s[t, b]]]
                mixed += mask_sc[t, b] * row[:, :rank_size]
            mixed = jnp.sum(mixed, axis=1, keepdims=True)
            far_term = jnp.sum(tgtb_ref[t] * mixed, axis=0, keepdims=True)
            fresh.append(rhs[t] - near_term[t] - far_term)
        density = fresh
    for t in range(clusters):
        out_ref[t : t + 1, :] = density[t]


def local(
    shape_coef,
    force_coef,
    near_cell,
    near_dest,
    near_slot,
    panel_centers,
    near_blocks,
    near_pick,
    src_basis,
    far_couple,
    far_src,
    far_rank,
    tgt_basis,
    cluster_slot,
):
    cells = lax.axis_size("cells")
    walls = lax.axis_size("wall")
    near = near_cell.shape[0]
    clusters, width = panel_centers.shape
    panels = width // 3
    group = walls * clusters
    harmonic_host = harmonics(ORDER)
    harmonic = jnp.asarray(harmonic_host, F32).astype(BF16)
    grid_points = harmonic_host.shape[0]
    padded = -(-grid_points // LANES) * LANES
    harmonic_t = jnp.asarray(
        np.pad(harmonic_host.T, ((0, 0), (0, padded - grid_points))), F32
    ).astype(BF16)
    surface = jnp.einsum(
        "qs,asc->aqc", harmonic, shape_coef, preferred_element_type=F32
    ).astype(BF16)
    smem = pl.BlockSpec(memory_space=pltpu.SMEM)
    vmem = pl.BlockSpec(memory_space=pltpu.VMEM)
    density = pl.pallas_call(
        functools.partial(wall_kernel, cells, walls),
        out_shape=jax.ShapeDtypeStruct((clusters, width), F32),
        in_specs=[smem] * 6 + [vmem] * 11,
        out_specs=vmem,
        scratch_shapes=[
            pltpu.VMEM((near, ROWS, 2 * padded), F32),
            pltpu.VMEM((group, panels, ROWS), BF16),
            pltpu.VMEM((ROWS, panels), F32),
            pltpu.VMEM((group, 1, width), F32),
            pltpu.VMEM((near * ROWS, panels), F32),
            pltpu.VMEM((group, 8, panels), F32),
            pltpu.VMEM((group, 1, width), F32),
            pltpu.VMEM((walls, clusters, 1, width), F32),
            pltpu.VMEM((ITERS, clusters, 1, width), F32),
            pltpu.VMEM(far_couple.shape, F32),
            pltpu.SemaphoreType.DMA((2 + ITERS, walls)),
            pltpu.SemaphoreType.DMA((2 + ITERS, walls)),
            pltpu.SemaphoreType.DMA((ITERS, cells)),
            pltpu.SemaphoreType.DMA((ITERS, cells)),
            pltpu.SemaphoreType.DMA((ITERS,)),
            pltpu.SemaphoreType.DMA((ITERS,)),
        ]
        + [
            pltpu.VMEM((cells * group, 1, LANES), F32),
            pltpu.VMEM((clusters, 1, width), F32),
        ]
        * ITERS,
        compiler_params=pltpu.CompilerParams(
            collective_id=0, has_side_effects=True, vmem_limit_bytes=48 * 1024 * 1024
        ),
    )(
        near_dest,
        near_slot,
        near_pick,
        far_src,
        far_rank,
        cluster_slot,
        near_cell[None, :],
        near_dest[None, :],
        near_slot[None, :],
        harmonic_t,
        shape_coef,
        force_coef,
        panel_centers,
        near_blocks,
        jnp.transpose(src_basis, (0, 2, 1)),
        far_couple,
        tgt_basis,
    )
    return (surface, density)


def solution(mesh):
    return jax.shard_map(
        local,
        mesh=mesh,
        in_specs=(
            P(None, None, ("cells", "wall")),
            P(None, None, ("cells", "wall")),
            P(("cells", "wall")),
            P(("cells", "wall")),
            P(("cells", "wall")),
            P(("cells", "wall"), None),
            P(("cells", "wall"), None, None, None),
            P(("cells", "wall")),
            P(("cells", "wall"), None, None),
            P(("cells", "wall"), None, None, None),
            P(("cells", "wall"), None),
            P(("cells", "wall"), None),
            P(("cells", "wall"), None, None),
            P(),
        ),
        out_specs=(P(None, None, ("cells", "wall")), P(("cells", "wall"), None)),
        check_vma=False,
    )
```

```python
import functools
import math

import jax
import jax.numpy as jnp
import numpy as np
from jax import lax
from jax.experimental import pallas as pl
from jax.experimental.pallas import tpu as pltpu
from jax.sharding import PartitionSpec as P

ORDER = 16
ITERS = 2
LANES = 128
ROWS = 16
SPAN = 256
OPERANDS = 17

soft_core = 0.25
stokes_scale = 1.0 / (8.0 * math.pi)

MESH = pl.DeviceIdType.MESH
HIGHEST = lax.Precision.HIGHEST
F32 = jnp.float32
BF16 = jnp.bfloat16
NT = (((1,), (1,)), ((), ()))


def harmonics(order):
    lat_count = order + 1
    polar_angle = np.pi * (np.arange(lat_count) + 0.5) / lat_count
    azimuth = np.pi * np.arange(2 * lat_count) / lat_count
    cos_polar = np.repeat(np.cos(polar_angle), 2 * lat_count)
    sin_polar = np.repeat(np.sin(polar_angle), 2 * lat_count)
    az_grid = np.tile(azimuth, lat_count)
    legendre = {}
    legendre[0, 0] = cos_polar * 0.0 + 0.5 / np.sqrt(np.pi)
    for m in range(1, order + 1):
        legendre[m, m] = -np.sqrt((2.0 * m + 1.0) / (2.0 * m)) * sin_polar * legendre[m - 1, m - 1]
    for m in range(order):
        legendre[m + 1, m] = np.sqrt(2.0 * m + 3.0) * cos_polar * legendre[m, m]
    for m in range(order + 1):
        for l in range(m + 2, order + 1):
            factor = np.sqrt((4.0 * l * l - 1.0) / (l * l - m * m))
            backward = np.sqrt(((l - 1.0) ** 2 - m * m) / (4.0 * (l - 1.0) ** 2 - 1.0))
            legendre[l, m] = factor * (
                cos_polar * legendre[l - 1, m] - backward * legendre[l - 2, m]
            )
    columns = []
    for l in range(order + 1):
        for m in range(-l, l + 1):
            if m > 0:
                columns.append(np.sqrt(2.0) * legendre[l, m] * np.cos(m * az_grid))
            elif m < 0:
                columns.append(np.sqrt(2.0) * legendre[l, -m] * np.sin(-m * az_grid))
            else:
                columns.append(legendre[l, 0])
    return np.stack(columns, axis=1)


def each(count, body):
    if count <= 16:
        for i in range(count):
            body(i)
    else:
        def step(i, carry):
            body(i)
            return carry

        lax.fori_loop(0, count, step, 0)


def rounded(value):
    return value.astype(BF16).astype(F32)


def split3(value):
    first = rounded(value)
    rest = value - first
    second = rounded(rest)
    return first, second, rounded(rest - second)


def wall_kernel(
    cells,
    walls,
    points_count,
    *refs,
):
    operands, refs = refs[:OPERANDS], refs[OPERANDS:]
    out_ref, refs = refs[0], refs[1:]
    held, refs = refs[:OPERANDS], refs[OPERANDS:]
    (
        b_sc,
        bt_sc,
        a_sc,
        at_sc,
        x_sc,
        v_sc,
        e_sc,
        s_sc,
        part_sc,
        recv_sc,
        stage_sc,
        mask_sc,
        load_sem,
        wall_send,
        wall_recv,
        cell_send,
        cell_recv,
        ring_send,
        ring_recv,
        *step_sc,
    ) = refs
    loads = [
        pltpu.make_async_copy(operands[i], held[i], load_sem.at[i]) for i in range(OPERANDS)
    ]
    (
        cell_ref,
        shape_ref,
        harm_ref,
        centers_ref,
        force_ref,
        dest_ref,
        slot_ref,
        dest_s,
        slot_s,
        rank_s,
        couple_ref,
        pick_s,
        src_s,
        owner_s,
        srcb_ref,
        tgtb_ref,
        blocks_ref,
    ) = held
    for load in loads:
        load.start()
    clusters = centers_ref.shape[0]
    panels = centers_ref.shape[1] // 3
    near = dest_ref.shape[1]
    group = walls * clusters
    padded = b_sc.shape[2]
    chunks = padded // LANES
    batch = LANES // (2 * ROWS)
    me_cell = lax.axis_index("cells")
    me = lax.axis_index("wall")

    def wall_peer(d):
        return lax.rem(me + d, walls)

    def cell_peer(d):
        return lax.rem(me_cell + d, cells)

    barrier = pltpu.get_barrier_semaphore()

    def greet_wall(i):
        pl.semaphore_signal(barrier, inc=1, device_id={"wall": wall_peer(i + 1)}, device_id_type=MESH)

    def greet_cell(i):
        pl.semaphore_signal(barrier, inc=1, device_id={"cells": cell_peer(i + 1)}, device_id_type=MESH)

    each(walls - 1, greet_wall)
    each(cells - 1, greet_cell)

    def column(row):
        size = row.shape[1]
        down = lax.broadcasted_iota(jnp.int32, (size, size), 0)
        across = lax.broadcasted_iota(jnp.int32, (size, size), 1)
        return jnp.sum(jnp.where(down == across, row, 0.0), axis=1, keepdims=True)

    a_sc[...] = jnp.zeros(a_sc.shape, BF16)
    for load in loads[:4]:
        load.wait()
    for s in range(clusters):
        x_sc[me * clusters + s] = centers_ref[s : s + 1, :]
    cell_col = column(cell_ref[...].astype(F32))
    cell_count = shape_ref.shape[2]
    lane_cell = lax.broadcasted_iota(jnp.int32, (near, cell_count), 1).astype(F32)
    onehot = (lane_cell == cell_col).astype(BF16)

    def on_grid(ref, a):
        picked = lax.dot_general(onehot, ref[a], NT, preferred_element_type=F32).astype(BF16)
        return rounded(jnp.dot(picked, harm_ref[...], preferred_element_type=F32))

    def put(row, half, value):
        b_sc[:, half * ROWS + row, :] = value

    points = [on_grid(shape_ref, a) for a in range(3)]

    pl.semaphore_wait(barrier, walls + cells - 2)

    def wall_copy(phase, d, src, dst):
        return pltpu.make_async_remote_copy(
            src_ref=src,
            dst_ref=dst,
            send_sem=wall_send.at[phase, d],
            recv_sem=wall_recv.at[phase, d],
            device_id={"wall": wall_peer(d)},
            device_id_type=MESH,
        )

    own = pl.ds(me * clusters, clusters)

    def center_copy(d):
        return wall_copy(0, d, x_sc.at[own], x_sc.at[own])

    each(walls - 1, lambda i: center_copy(i + 1).start())

    for load in loads[4:]:
        load.wait()
    forces = [on_grid(force_ref, a) for a in range(3)]
    zero = jnp.zeros_like(points[0])
    one = zero + 1.0
    square = points[0] * points[0] + points[1] * points[1] + points[2] * points[2] + soft_core
    inner = points[0] * forces[0] + points[1] * forces[1] + points[2] * forces[2]
    for a in range(3):
        double = points[a] * -2.0
        for half, value in ((0, double), (1, forces[a])):
            put(a, half, value)
            put(12 + a, half, value)
        put(8 + a, 0, points[a])
        put(8 + a, 1, zero)
        put(3 + a, 0, one)
        put(3 + a, 1, zero)
    for row, sq, inn in zip((6, 7, 15), split3(square), split3(inner)):
        put(row, 0, sq)
        put(row, 1, -inn)
    put(11, 0, zero)
    put(11, 1, zero)

    def turn(g, carry):
        for j in range(chunks):
            width = min(LANES, points_count - j * LANES)
            tile = b_sc[pl.ds(g * batch, batch), :, j * LANES : (j + 1) * LANES]
            turned = jnp.transpose(tile.reshape(LANES, LANES))
            bt_sc[g, j * LANES : j * LANES + width, :] = turned[:width].astype(BF16)
        return carry

    lax.fori_loop(0, near // batch, turn, 0)

    rank_size = couple_ref.shape[2]
    far_blocks = couple_ref.shape[1]
    level_i = lax.broadcasted_iota(jnp.int32, (rank_size, rank_size), 0)
    level_j = lax.broadcasted_iota(jnp.int32, (rank_size, rank_size), 1)
    level = jnp.maximum(level_i, level_j)
    for t in range(clusters):
        for b in range(far_blocks):
            mask_sc[t, b] = jnp.where(level < rank_s[t, b], couple_ref[t, b], 0.0)

    flat = near * 8
    target_row = (dest_ref[...] * clusters + slot_ref[...]).astype(F32)
    spread = (
        lax.shift_right_logical(lax.broadcasted_iota(jnp.int32, (near, flat), 1), 3)
        == lax.broadcasted_iota(jnp.int32, (near, flat), 0)
    ).astype(F32)
    target_flat = jnp.dot(
        jnp.broadcast_to(target_row, (8, near)), spread, precision=HIGHEST, preferred_element_type=F32
    )[0:1]
    down = lax.broadcasted_iota(jnp.int32, (group * 8, flat), 0)
    across = lax.broadcasted_iota(jnp.int32, (group * 8, flat), 1)
    same = lax.shift_right_logical(down, 3).astype(F32) == target_flat
    e_sc[...] = jnp.where(same & ((down & 7) == (across & 7)), 1.0, 0.0).astype(BF16)

    at_sc[6:12, :] = jnp.ones((6, panels), F32)
    at_sc[8:12, :] = jnp.zeros((4, panels), F32)
    at_sc[15:16, :] = jnp.ones((1, panels), F32)
    each(walls - 1, lambda i: center_copy(i + 1).wait())

    def make_panels(t):
        for a in range(3):
            spot = x_sc[t][:, a * panels : (a + 1) * panels]
            first = rounded(spot)
            second = rounded(spot - first)
            whole = first + second
            at_sc[a : a + 1, :] = first
            at_sc[12 + a : 13 + a, :] = second
            norm = whole * whole if a == 0 else norm + whole * whole
        for a, value in enumerate(split3(norm)):
            at_sc[3 + a : 4 + a, :] = value
        rows = at_sc[...].astype(BF16)
        a_sc[t, 0:ROWS, 0:panels] = rows
        a_sc[t, ROWS : 2 * ROWS, panels : 2 * panels] = rows

    each(group, make_panels)

    empty = jnp.zeros((2 * ROWS, 2 * panels), BF16)

    def pair_rows(g, carry):
        for i in range(batch):
            r = g * batch + i
            panel = a_sc[dest_s[r] * clusters + slot_s[r]]
            weights = jnp.concatenate([panel if k == i else empty for k in range(batch)], axis=0)
            rows = b_sc[r].astype(BF16)
            total = jnp.zeros((2 * ROWS, 2 * panels), F32)
            for start in range(0, points_count, SPAN):
                stop = min(start + SPAN, points_count)
                both = jnp.dot(bt_sc[g, start:stop, :], weights, preferred_element_type=F32)
                inverse = lax.rsqrt(both[:, :panels])
                along = both[:, panels:] * (inverse * inverse * inverse)
                pair = jnp.concatenate([along.astype(BF16), inverse.astype(BF16)], axis=1)
                total += jnp.dot(rows[:, start:stop], pair, preferred_element_type=F32)
            summed = total[:ROWS, :panels] + total[ROWS:, panels:]
            v_sc[pl.ds(pl.multiple_of(r * 8, 8), 8), :] = summed[:8] + summed[8:]
        return carry

    lax.fori_loop(0, near // batch, pair_rows, 0)

    value = v_sc[...]
    high = value.astype(BF16)
    low_part = (value - high.astype(F32)).astype(BF16)
    select = e_sc[...]
    s_sc[...] = (
        jnp.dot(select, high, preferred_element_type=F32)
        + jnp.dot(select, low_part, preferred_element_type=F32)
    ).reshape(group, 8, panels)

    def make_part(t):
        for a in range(3):
            lanes = slice(a * panels, (a + 1) * panels)
            part_sc[t, :, lanes] = -stokes_scale * (
                s_sc[t, a : a + 1, :] + x_sc[t, :, lanes] * s_sc[t, 3:4, :]
            )

    each(group, make_part)

    def part_copy(d):
        return wall_copy(
            1, d, part_sc.at[pl.ds(wall_peer(d) * clusters, clusters)], recv_sc.at[me]
        )

    each(walls - 1, lambda i: part_copy(i + 1).start())
    recv_sc[me] = part_sc[own]
    each(walls - 1, lambda i: part_copy(i + 1).wait())
    total = jnp.sum(recv_sc[...], axis=0)
    rhs = [total[t] for t in range(clusters)]

    flat_i = lax.broadcasted_iota(jnp.int32, (rank_size, LANES), 0)
    flat_j = lax.broadcasted_iota(jnp.int32, (rank_size, LANES), 1)
    diagonal = flat_i == flat_j
    first_row = me_cell * group

    def apply_block(t, b, vector):
        low = jnp.broadcast_to(vector.astype(BF16), (ROWS, vector.shape[1]))
        return lax.dot_general(low, blocks_ref[t, b], NT, preferred_element_type=F32)[0:1]

    density = rhs
    for step in range(ITERS):
        table_sc, nbr_sc = step_sc[2 * step : 2 * step + 2]
        ring = pltpu.make_async_remote_copy(
            src_ref=stage_sc.at[step],
            dst_ref=nbr_sc,
            send_sem=ring_send.at[step],
            recv_sem=ring_recv.at[step],
            device_id={"wall": wall_peer(1)},
            device_id_type=MESH,
        )
        for t in range(clusters):
            coef = jnp.sum(srcb_ref[t] * density[t], axis=1, keepdims=True)
            table_sc[first_row + me * clusters + t] = jnp.sum(
                jnp.where(diagonal, coef, 0.0), axis=0, keepdims=True
            )
            stage_sc[step, t] = density[t]
        mine = table_sc.at[pl.ds(first_row + me * clusters, clusters)]

        def coef_copy(d):
            return wall_copy(2 + step, d, mine, mine)

        each(walls - 1, lambda i: coef_copy(i + 1).start())
        ring.start()
        near_term = [apply_block(t, 0, density[t]) for t in range(clusters)]
        each(walls - 1, lambda i: coef_copy(i + 1).wait())
        block = table_sc.at[pl.ds(first_row, group)]

        def block_copy(d):
            return pltpu.make_async_remote_copy(
                src_ref=block,
                dst_ref=block,
                send_sem=cell_send.at[step, d],
                recv_sem=cell_recv.at[step, d],
                device_id={"cells": cell_peer(d)},
                device_id_type=MESH,
            )

        each(cells - 1, lambda i: block_copy(i + 1).start())
        ring.wait()
        near_term = [
            near_term[t] + apply_block(t, 1, nbr_sc[pick_s[t]]) for t in range(clusters)
        ]
        each(cells - 1, lambda i: block_copy(i + 1).wait())
        fresh = []
        for t in range(clusters):
            mixed = jnp.zeros((rank_size, rank_size), F32)
            for b in range(far_blocks):
                row = table_sc[owner_s[src_s[t, b]]]
                mixed += mask_sc[t, b] * row[:, :rank_size]
            mixed = jnp.sum(mixed, axis=1, keepdims=True)
            far_term = jnp.sum(tgtb_ref[t] * mixed, axis=0, keepdims=True)
            fresh.append(rhs[t] - near_term[t] - far_term)
        density = fresh
    for t in range(clusters):
        out_ref[t : t + 1, :] = density[t]


def local(
    shape_coef,
    force_coef,
    near_cell,
    near_dest,
    near_slot,
    panel_centers,
    near_blocks,
    near_pick,
    src_basis,
    far_couple,
    far_src,
    far_rank,
    tgt_basis,
    cluster_slot,
):
    cells = lax.axis_size("cells")
    walls = lax.axis_size("wall")
    near = near_cell.shape[0]
    clusters, width = panel_centers.shape
    panels = width // 3
    group = walls * clusters
    harmonic_host = harmonics(ORDER)
    harmonic = jnp.asarray(harmonic_host, F32).astype(BF16)
    grid_points = harmonic_host.shape[0]
    padded = -(-grid_points // LANES) * LANES
    harmonic_t = jnp.asarray(
        np.pad(harmonic_host.T, ((0, 0), (0, padded - grid_points))), F32
    ).astype(BF16)
    surface = jnp.einsum(
        "qs,asc->aqc", harmonic, shape_coef, preferred_element_type=F32
    ).astype(BF16)
    points_count = -(-grid_points // 16) * 16
    operands = (
        near_cell[None, :],
        shape_coef,
        harmonic_t,
        panel_centers,
        force_coef,
        near_dest[None, :],
        near_slot[None, :],
        near_dest,
        near_slot,
        far_rank,
        far_couple,
        near_pick,
        far_src,
        cluster_slot,
        jnp.transpose(src_basis, (0, 2, 1)),
        tgt_basis,
        near_blocks,
    )
    scalars = (7, 8, 9, 11, 12, 13)
    density = pl.pallas_call(
        functools.partial(wall_kernel, cells, walls, points_count),
        out_shape=jax.ShapeDtypeStruct((clusters, width), F32),
        in_specs=[pl.BlockSpec(memory_space=pltpu.HBM)] * OPERANDS,
        out_specs=pl.BlockSpec(memory_space=pltpu.VMEM),
        scratch_shapes=[
            (pltpu.SMEM if i in scalars else pltpu.VMEM)(array.shape, array.dtype)
            for i, array in enumerate(operands)
        ]
        + [
            pltpu.VMEM((near, 2 * ROWS, padded), F32),
            pltpu.VMEM((near * 2 * ROWS // LANES, points_count, LANES), BF16),
            pltpu.VMEM((group, 2 * ROWS, 2 * panels), BF16),
            pltpu.VMEM((ROWS, panels), F32),
            pltpu.VMEM((group, 1, width), F32),
            pltpu.VMEM((near * 8, panels), F32),
            pltpu.VMEM((group * 8, near * 8), BF16),
            pltpu.VMEM((group, 8, panels), F32),
            pltpu.VMEM((group, 1, width), F32),
            pltpu.VMEM((walls, clusters, 1, width), F32),
            pltpu.VMEM((ITERS, clusters, 1, width), F32),
            pltpu.VMEM(far_couple.shape, F32),
            pltpu.SemaphoreType.DMA((OPERANDS,)),
            pltpu.SemaphoreType.DMA((2 + ITERS, walls)),
            pltpu.SemaphoreType.DMA((2 + ITERS, walls)),
            pltpu.SemaphoreType.DMA((ITERS, cells)),
            pltpu.SemaphoreType.DMA((ITERS, cells)),
            pltpu.SemaphoreType.DMA((ITERS,)),
            pltpu.SemaphoreType.DMA((ITERS,)),
        ]
        + [
            pltpu.VMEM((cells * group, 1, LANES), F32),
            pltpu.VMEM((clusters, 1, width), F32),
        ]
        * ITERS,
        compiler_params=pltpu.CompilerParams(
            collective_id=0, has_side_effects=True, vmem_limit_bytes=60 * 1024 * 1024
        ),
    )(*operands)
    return (surface, density)


def solution(mesh):
    return jax.shard_map(
        local,
        mesh=mesh,
        in_specs=(
            P(None, None, ("cells", "wall")),
            P(None, None, ("cells", "wall")),
            P(("cells", "wall")),
            P(("cells", "wall")),
            P(("cells", "wall")),
            P(("cells", "wall"), None),
            P(("cells", "wall"), None, None, None),
            P(("cells", "wall")),
            P(("cells", "wall"), None, None),
            P(("cells", "wall"), None, None, None),
            P(("cells", "wall"), None),
            P(("cells", "wall"), None),
            P(("cells", "wall"), None, None),
            P(),
        ),
        out_specs=(P(None, None, ("cells", "wall")), P(("cells", "wall"), None)),
        check_vma=False,
    )
```

```python
import functools
import math

import jax
import jax.numpy as jnp
import numpy as np
from jax import lax
from jax.experimental import pallas as pl
from jax.experimental.pallas import tpu as pltpu
from jax.sharding import PartitionSpec as P

ORDER = 16
ITERS = 2
LANES = 128
ROWS = 16
SPAN = 256
OPERANDS = 17

soft_core = 0.25
stokes_scale = 1.0 / (8.0 * math.pi)

MESH = pl.DeviceIdType.MESH
HIGHEST = lax.Precision.HIGHEST
F32 = jnp.float32
BF16 = jnp.bfloat16
NT = (((1,), (1,)), ((), ()))


def harmonics(order):
    lat_count = order + 1
    polar_angle = np.pi * (np.arange(lat_count) + 0.5) / lat_count
    azimuth = np.pi * np.arange(2 * lat_count) / lat_count
    cos_polar = np.repeat(np.cos(polar_angle), 2 * lat_count)
    sin_polar = np.repeat(np.sin(polar_angle), 2 * lat_count)
    az_grid = np.tile(azimuth, lat_count)
    legendre = {}
    legendre[0, 0] = cos_polar * 0.0 + 0.5 / np.sqrt(np.pi)
    for m in range(1, order + 1):
        legendre[m, m] = -np.sqrt((2.0 * m + 1.0) / (2.0 * m)) * sin_polar * legendre[m - 1, m - 1]
    for m in range(order):
        legendre[m + 1, m] = np.sqrt(2.0 * m + 3.0) * cos_polar * legendre[m, m]
    for m in range(order + 1):
        for l in range(m + 2, order + 1):
            factor = np.sqrt((4.0 * l * l - 1.0) / (l * l - m * m))
            backward = np.sqrt(((l - 1.0) ** 2 - m * m) / (4.0 * (l - 1.0) ** 2 - 1.0))
            legendre[l, m] = factor * (
                cos_polar * legendre[l - 1, m] - backward * legendre[l - 2, m]
            )
    columns = []
    for l in range(order + 1):
        for m in range(-l, l + 1):
            if m > 0:
                columns.append(np.sqrt(2.0) * legendre[l, m] * np.cos(m * az_grid))
            elif m < 0:
                columns.append(np.sqrt(2.0) * legendre[l, -m] * np.sin(-m * az_grid))
            else:
                columns.append(legendre[l, 0])
    return np.stack(columns, axis=1)


def each(count, body):
    if count <= 32:
        for i in range(count):
            body(i)
    else:
        def step(i, carry):
            body(i)
            return carry

        lax.fori_loop(0, count, step, 0)


def rounded(value):
    return value.astype(BF16).astype(F32)


def split3(value):
    first = rounded(value)
    rest = value - first
    second = rounded(rest)
    return first, second, rounded(rest - second)


def wall_kernel(
    cells,
    walls,
    points_count,
    *refs,
):
    operands, refs = refs[:OPERANDS], refs[OPERANDS:]
    out_ref, refs = refs[0], refs[1:]
    held, refs = refs[:OPERANDS], refs[OPERANDS:]
    (
        b_sc,
        bt_sc,
        a_sc,
        at_sc,
        x_sc,
        v_sc,
        e_sc,
        s_sc,
        part_sc,
        recv_sc,
        stage_sc,
        mask_sc,
        load_sem,
        wall_send,
        wall_recv,
        cell_send,
        cell_recv,
        ring_send,
        ring_recv,
        *step_sc,
    ) = refs
    loads = [
        pltpu.make_async_copy(operands[i], held[i], load_sem.at[i]) for i in range(OPERANDS)
    ]
    (
        cell_ref,
        shape_ref,
        harm_ref,
        centers_ref,
        force_ref,
        dest_ref,
        slot_ref,
        dest_s,
        slot_s,
        rank_s,
        couple_ref,
        pick_s,
        src_s,
        owner_s,
        srcb_ref,
        tgtb_ref,
        blocks_ref,
    ) = held
    for load in loads:
        load.start()
    clusters = centers_ref.shape[0]
    panels = centers_ref.shape[1] // 3
    near = dest_ref.shape[1]
    group = walls * clusters
    padded = b_sc.shape[2]
    chunks = padded // LANES
    batch = LANES // (2 * ROWS)
    me_cell = lax.axis_index("cells")
    me = lax.axis_index("wall")

    def wall_peer(d):
        return lax.rem(me + d, walls)

    def cell_peer(d):
        return lax.rem(me_cell + d, cells)

    barrier = pltpu.get_barrier_semaphore()

    def greet_wall(i):
        pl.semaphore_signal(barrier, inc=1, device_id={"wall": wall_peer(i + 1)}, device_id_type=MESH)

    def greet_cell(i):
        pl.semaphore_signal(barrier, inc=1, device_id={"cells": cell_peer(i + 1)}, device_id_type=MESH)

    devices = cells * walls
    direct = devices <= 64

    def any_peer(d):
        peer = lax.rem(me_cell * walls + me + d, devices)
        return {"cells": lax.div(peer, walls), "wall": lax.rem(peer, walls)}

    def greet_any(i):
        pl.semaphore_signal(barrier, inc=1, device_id=any_peer(i + 1), device_id_type=MESH)

    if direct:
        each(devices - 1, greet_any)
    else:
        each(walls - 1, greet_wall)
        each(cells - 1, greet_cell)

    def column(row):
        size = row.shape[1]
        down = lax.broadcasted_iota(jnp.int32, (size, size), 0)
        across = lax.broadcasted_iota(jnp.int32, (size, size), 1)
        return jnp.sum(jnp.where(down == across, row, 0.0), axis=1, keepdims=True)

    a_sc[...] = jnp.zeros(a_sc.shape, BF16)
    for load in loads[:4]:
        load.wait()
    for s in range(clusters):
        x_sc[me * clusters + s] = centers_ref[s : s + 1, :]
    cell_col = column(cell_ref[...].astype(F32))
    cell_count = shape_ref.shape[2]
    lane_cell = lax.broadcasted_iota(jnp.int32, (near, cell_count), 1).astype(F32)
    onehot = (lane_cell == cell_col).astype(BF16)

    def pick(ref):
        return [
            lax.dot_general(onehot, ref[a], NT, preferred_element_type=F32).astype(BF16)
            for a in range(3)
        ]

    def put(row, half, value):
        b_sc[:, half * ROWS + row, :] = value

    picked = pick(shape_ref)

    pl.semaphore_wait(barrier, devices - 1 if direct else walls + cells - 2)

    def wall_copy(phase, d, src, dst):
        return pltpu.make_async_remote_copy(
            src_ref=src,
            dst_ref=dst,
            send_sem=wall_send.at[phase, d],
            recv_sem=wall_recv.at[phase, d],
            device_id={"wall": wall_peer(d)},
            device_id_type=MESH,
        )

    own = pl.ds(me * clusters, clusters)

    def center_copy(d):
        return wall_copy(0, d, x_sc.at[own], x_sc.at[own])

    each(walls - 1, lambda i: center_copy(i + 1).start())

    for load in loads[4:]:
        load.wait()
    picked = jnp.concatenate(picked + pick(force_ref), axis=0)
    grid = rounded(jnp.dot(picked, harm_ref[...], preferred_element_type=F32))
    points = [grid[a * near : (a + 1) * near] for a in range(3)]
    forces = [grid[a * near : (a + 1) * near] for a in range(3, 6)]
    zero = jnp.zeros_like(points[0])
    one = zero + 1.0
    square = points[0] * points[0] + points[1] * points[1] + points[2] * points[2] + soft_core
    inner = points[0] * forces[0] + points[1] * forces[1] + points[2] * forces[2]
    for a in range(3):
        double = points[a] * -2.0
        for half, value in ((0, double), (1, forces[a])):
            put(a, half, value)
            put(12 + a, half, value)
        put(8 + a, 0, points[a])
        put(8 + a, 1, zero)
        put(3 + a, 0, one)
        put(3 + a, 1, zero)
    for row, sq, inn in zip((6, 7, 15), split3(square), split3(inner)):
        put(row, 0, sq)
        put(row, 1, -inn)
    put(11, 0, zero)
    put(11, 1, zero)

    def turn(g, carry):
        for j in range(chunks):
            width = min(LANES, points_count - j * LANES)
            tile = b_sc[pl.ds(g * batch, batch), :, j * LANES : (j + 1) * LANES]
            turned = jnp.transpose(tile.reshape(LANES, LANES).astype(BF16))
            bt_sc[g, j * LANES : j * LANES + width, :] = turned[:width]
        return carry

    lax.fori_loop(0, near // batch, turn, 0)

    rank_size = couple_ref.shape[2]
    far_blocks = couple_ref.shape[1]
    level_i = lax.broadcasted_iota(jnp.int32, (rank_size, rank_size), 0)
    level_j = lax.broadcasted_iota(jnp.int32, (rank_size, rank_size), 1)
    level = jnp.maximum(level_i, level_j)
    for t in range(clusters):
        for b in range(far_blocks):
            mask_sc[t, b] = jnp.where(level < rank_s[t, b], couple_ref[t, b], 0.0)

    flat = near * 8
    target_row = (dest_ref[...] * clusters + slot_ref[...]).astype(F32)
    spread = (
        lax.shift_right_logical(lax.broadcasted_iota(jnp.int32, (near, flat), 1), 3)
        == lax.broadcasted_iota(jnp.int32, (near, flat), 0)
    ).astype(F32)
    target_flat = jnp.dot(
        jnp.broadcast_to(target_row, (8, near)), spread, precision=HIGHEST, preferred_element_type=F32
    )[0:1]
    down = lax.broadcasted_iota(jnp.int32, (group * 8, flat), 0)
    across = lax.broadcasted_iota(jnp.int32, (group * 8, flat), 1)
    same = lax.shift_right_logical(down, 3).astype(F32) == target_flat
    e_sc[...] = jnp.where(same & ((down & 7) == (across & 7)), 1.0, 0.0).astype(BF16)

    kind = lax.broadcasted_iota(jnp.int32, (group, ROWS, panels), 1)
    at_sc[...] = jnp.where((kind == 6) | (kind == 7) | (kind == 15), 1.0, 0.0)
    each(walls - 1, lambda i: center_copy(i + 1).wait())

    def make_panels(t):
        for a in range(3):
            spot = x_sc[t][:, a * panels : (a + 1) * panels]
            first = rounded(spot)
            second = rounded(spot - first)
            whole = first + second
            at_sc[t, a : a + 1, :] = first
            at_sc[t, 12 + a : 13 + a, :] = second
            norm = whole * whole if a == 0 else norm + whole * whole
        for a, value in enumerate(split3(norm)):
            at_sc[t, 3 + a : 4 + a, :] = value
        rows = at_sc[t].astype(BF16)
        a_sc[t, 0:ROWS, 0:panels] = rows
        a_sc[t, ROWS : 2 * ROWS, panels : 2 * panels] = rows

    each(group, make_panels)

    empty = jnp.zeros((2 * ROWS, 2 * panels), BF16)

    def pair_rows(g, carry):
        for i in range(batch):
            r = g * batch + i
            panel = a_sc[dest_s[r] * clusters + slot_s[r]]
            weights = jnp.concatenate([panel if k == i else empty for k in range(batch)], axis=0)
            rows = b_sc[r].astype(BF16)
            total = jnp.zeros((2 * ROWS, 2 * panels), F32)
            whole = jnp.dot(bt_sc[g], weights, preferred_element_type=F32)
            for start in range(0, points_count, SPAN):
                stop = min(start + SPAN, points_count)
                both = whole[start:stop]
                inverse = lax.rsqrt(both[:, :panels])
                along = both[:, panels:] * (inverse * inverse * inverse)
                pair = jnp.concatenate([along.astype(BF16), inverse.astype(BF16)], axis=1)
                total += jnp.dot(rows[:, start:stop], pair, preferred_element_type=F32)
            summed = total[:ROWS, :panels] + total[ROWS:, panels:]
            v_sc[pl.ds(pl.multiple_of(r * 8, 8), 8), :] = summed[:8] + summed[8:]
        return carry

    lax.fori_loop(0, near // batch, pair_rows, 0)

    value = v_sc[...]
    high = value.astype(BF16)
    low_part = (value - high.astype(F32)).astype(BF16)
    select = e_sc[...]
    s_sc[...] = (
        jnp.dot(select, high, preferred_element_type=F32)
        + jnp.dot(select, low_part, preferred_element_type=F32)
    ).reshape(group, 8, panels)

    def make_part(t):
        for a in range(3):
            lanes = slice(a * panels, (a + 1) * panels)
            part_sc[t, :, lanes] = -stokes_scale * (
                s_sc[t, a : a + 1, :] + x_sc[t, :, lanes] * s_sc[t, 3:4, :]
            )

    each(group, make_part)

    def part_copy(d):
        return wall_copy(
            1, d, part_sc.at[pl.ds(wall_peer(d) * clusters, clusters)], recv_sc.at[me]
        )

    each(walls - 1, lambda i: part_copy(i + 1).start())
    recv_sc[me] = part_sc[own]
    each(walls - 1, lambda i: part_copy(i + 1).wait())
    total = jnp.sum(recv_sc[...], axis=0)
    rhs = [total[t] for t in range(clusters)]

    flat_i = lax.broadcasted_iota(jnp.int32, (rank_size, LANES), 0)
    flat_j = lax.broadcasted_iota(jnp.int32, (rank_size, LANES), 1)
    diagonal = flat_i == flat_j
    first_row = me_cell * group

    def apply_block(t, b, vector):
        low = jnp.broadcast_to(vector.astype(BF16), (ROWS, vector.shape[1]))
        return lax.dot_general(low, blocks_ref[t, b], NT, preferred_element_type=F32)[0:1]

    density = rhs
    for step in range(ITERS):
        table_sc, nbr_sc = step_sc[2 * step : 2 * step + 2]
        ring = pltpu.make_async_remote_copy(
            src_ref=stage_sc.at[step],
            dst_ref=nbr_sc,
            send_sem=ring_send.at[step],
            recv_sem=ring_recv.at[step],
            device_id={"wall": wall_peer(1)},
            device_id_type=MESH,
        )
        for t in range(clusters):
            coef = jnp.sum(srcb_ref[t] * density[t], axis=1, keepdims=True)
            table_sc[first_row + me * clusters + t] = jnp.sum(
                jnp.where(diagonal, coef, 0.0), axis=0, keepdims=True
            )
            stage_sc[step, t] = density[t]
        mine = table_sc.at[pl.ds(first_row + me * clusters, clusters)]

        def coef_copy(d):
            return wall_copy(2 + step, d, mine, mine)

        def any_copy(d, rows):
            return pltpu.make_async_remote_copy(
                src_ref=rows,
                dst_ref=rows,
                send_sem=cell_send.at[step, 0],
                recv_sem=cell_recv.at[step, 0],
                device_id=any_peer(d),
                device_id_type=MESH,
            )

        block = table_sc.at[pl.ds(first_row, group)]

        def block_copy(d):
            return pltpu.make_async_remote_copy(
                src_ref=block,
                dst_ref=block,
                send_sem=cell_send.at[step, d],
                recv_sem=cell_recv.at[step, d],
                device_id={"cells": cell_peer(d)},
                device_id_type=MESH,
            )

        ring.start()
        if direct:
            each(devices - 1, lambda i: any_copy(i + 1, mine).start())
        else:
            each(walls - 1, lambda i: coef_copy(i + 1).start())
        near_term = [apply_block(t, 0, density[t]) for t in range(clusters)]
        if not direct:
            each(walls - 1, lambda i: coef_copy(i + 1).wait())
            each(cells - 1, lambda i: block_copy(i + 1).start())
        ring.wait()
        near_term = [
            near_term[t] + apply_block(t, 1, nbr_sc[pick_s[t]]) for t in range(clusters)
        ]
        if direct:
            any_copy(1, table_sc.at[pl.ds(0, (devices - 1) * clusters)]).wait()
        else:
            each(cells - 1, lambda i: block_copy(i + 1).wait())
        fresh = []
        for t in range(clusters):
            mixed = jnp.zeros((rank_size, rank_size), F32)
            for b in range(far_blocks):
                row = table_sc[owner_s[src_s[t, b]]]
                mixed += mask_sc[t, b] * row[:, :rank_size]
            mixed = jnp.sum(mixed, axis=1, keepdims=True)
            far_term = jnp.sum(tgtb_ref[t] * mixed, axis=0, keepdims=True)
            fresh.append(rhs[t] - near_term[t] - far_term)
        density = fresh
    for t in range(clusters):
        out_ref[t : t + 1, :] = density[t]


def local(
    shape_coef,
    force_coef,
    near_cell,
    near_dest,
    near_slot,
    panel_centers,
    near_blocks,
    near_pick,
    src_basis,
    far_couple,
    far_src,
    far_rank,
    tgt_basis,
    cluster_slot,
):
    cells = lax.axis_size("cells")
    walls = lax.axis_size("wall")
    near = near_cell.shape[0]
    clusters, width = panel_centers.shape
    panels = width // 3
    group = walls * clusters
    harmonic_host = harmonics(ORDER)
    harmonic = jnp.asarray(harmonic_host, F32).astype(BF16)
    grid_points = harmonic_host.shape[0]
    padded = -(-grid_points // LANES) * LANES
    harmonic_t = jnp.asarray(
        np.pad(harmonic_host.T, ((0, 0), (0, padded - grid_points))), F32
    ).astype(BF16)
    surface = jnp.einsum(
        "qs,asc->aqc", harmonic, shape_coef, preferred_element_type=F32
    ).astype(BF16)
    points_count = -(-grid_points // 16) * 16
    operands = (
        near_cell[None, :],
        shape_coef,
        harmonic_t,
        panel_centers,
        force_coef,
        near_dest[None, :],
        near_slot[None, :],
        near_dest,
        near_slot,
        far_rank,
        far_couple,
        near_pick,
        far_src,
        cluster_slot,
        jnp.transpose(src_basis, (0, 2, 1)),
        tgt_basis,
        near_blocks,
    )
    scalars = (7, 8, 9, 11, 12, 13)
    density = pl.pallas_call(
        functools.partial(wall_kernel, cells, walls, points_count),
        out_shape=jax.ShapeDtypeStruct((clusters, width), F32),
        in_specs=[pl.BlockSpec(memory_space=pltpu.HBM)] * OPERANDS,
        out_specs=pl.BlockSpec(memory_space=pltpu.VMEM),
        scratch_shapes=[
            (pltpu.SMEM if i in scalars else pltpu.VMEM)(array.shape, array.dtype)
            for i, array in enumerate(operands)
        ]
        + [
            pltpu.VMEM((near, 2 * ROWS, padded), F32),
            pltpu.VMEM((near * 2 * ROWS // LANES, points_count, LANES), BF16),
            pltpu.VMEM((group, 2 * ROWS, 2 * panels), BF16),
            pltpu.VMEM((group, ROWS, panels), F32),
            pltpu.VMEM((group, 1, width), F32),
            pltpu.VMEM((near * 8, panels), F32),
            pltpu.VMEM((group * 8, near * 8), BF16),
            pltpu.VMEM((group, 8, panels), F32),
            pltpu.VMEM((group, 1, width), F32),
            pltpu.VMEM((walls, clusters, 1, width), F32),
            pltpu.VMEM((ITERS, clusters, 1, width), F32),
            pltpu.VMEM(far_couple.shape, F32),
            pltpu.SemaphoreType.DMA((OPERANDS,)),
            pltpu.SemaphoreType.DMA((2 + ITERS, walls)),
            pltpu.SemaphoreType.DMA((2 + ITERS, walls)),
            pltpu.SemaphoreType.DMA((ITERS, cells)),
            pltpu.SemaphoreType.DMA((ITERS, cells)),
            pltpu.SemaphoreType.DMA((ITERS,)),
            pltpu.SemaphoreType.DMA((ITERS,)),
        ]
        + [
            pltpu.VMEM((cells * group, 1, LANES), F32),
            pltpu.VMEM((clusters, 1, width), F32),
        ]
        * ITERS,
        compiler_params=pltpu.CompilerParams(
            collective_id=0, has_side_effects=True, vmem_limit_bytes=60 * 1024 * 1024
        ),
    )(*operands)
    return (surface, density)


def solution(mesh):
    return jax.shard_map(
        local,
        mesh=mesh,
        in_specs=(
            P(None, None, ("cells", "wall")),
            P(None, None, ("cells", "wall")),
            P(("cells", "wall")),
            P(("cells", "wall")),
            P(("cells", "wall")),
            P(("cells", "wall"), None),
            P(("cells", "wall"), None, None, None),
            P(("cells", "wall")),
            P(("cells", "wall"), None, None),
            P(("cells", "wall"), None, None, None),
            P(("cells", "wall"), None),
            P(("cells", "wall"), None),
            P(("cells", "wall"), None, None),
            P(),
        ),
        out_specs=(P(None, None, ("cells", "wall")), P(("cells", "wall"), None)),
        check_vma=False,
    )
```

```python
import functools
import math

import jax
import jax.numpy as jnp
import numpy as np
from jax import lax
from jax.experimental import pallas as pl
from jax.experimental.pallas import tpu as pltpu
from jax.sharding import PartitionSpec as P

ORDER = 16
ITERS = 2
LANES = 128
ROWS = 16
SPAN = 256
OPERANDS = 17

soft_core = 0.25
stokes_scale = 1.0 / (8.0 * math.pi)

MESH = pl.DeviceIdType.MESH
HIGHEST = lax.Precision.HIGHEST
F32 = jnp.float32
BF16 = jnp.bfloat16
NT = (((1,), (1,)), ((), ()))


def harmonics(order):
    lat_count = order + 1
    polar_angle = np.pi * (np.arange(lat_count) + 0.5) / lat_count
    azimuth = np.pi * np.arange(2 * lat_count) / lat_count
    cos_polar = np.repeat(np.cos(polar_angle), 2 * lat_count)
    sin_polar = np.repeat(np.sin(polar_angle), 2 * lat_count)
    az_grid = np.tile(azimuth, lat_count)
    legendre = {}
    legendre[0, 0] = cos_polar * 0.0 + 0.5 / np.sqrt(np.pi)
    for m in range(1, order + 1):
        legendre[m, m] = -np.sqrt((2.0 * m + 1.0) / (2.0 * m)) * sin_polar * legendre[m - 1, m - 1]
    for m in range(order):
        legendre[m + 1, m] = np.sqrt(2.0 * m + 3.0) * cos_polar * legendre[m, m]
    for m in range(order + 1):
        for l in range(m + 2, order + 1):
            factor = np.sqrt((4.0 * l * l - 1.0) / (l * l - m * m))
            backward = np.sqrt(((l - 1.0) ** 2 - m * m) / (4.0 * (l - 1.0) ** 2 - 1.0))
            legendre[l, m] = factor * (
                cos_polar * legendre[l - 1, m] - backward * legendre[l - 2, m]
            )
    columns = []
    for l in range(order + 1):
        for m in range(-l, l + 1):
            if m > 0:
                columns.append(np.sqrt(2.0) * legendre[l, m] * np.cos(m * az_grid))
            elif m < 0:
                columns.append(np.sqrt(2.0) * legendre[l, -m] * np.sin(-m * az_grid))
            else:
                columns.append(legendre[l, 0])
    return np.stack(columns, axis=1)


def each(count, body):
    if count <= 32:
        for i in range(count):
            body(i)
    else:
        def step(i, carry):
            body(i)
            return carry

        lax.fori_loop(0, count, step, 0)


def rounded(value):
    return value.astype(BF16).astype(F32)


def split3(value):
    first = rounded(value)
    rest = value - first
    second = rounded(rest)
    return first, second, rounded(rest - second)


def wall_kernel(
    cells,
    walls,
    points_count,
    *refs,
):
    operands, refs = refs[:OPERANDS], refs[OPERANDS:]
    out_ref, refs = refs[0], refs[1:]
    held, refs = refs[:OPERANDS], refs[OPERANDS:]
    (
        b_sc,
        bt_sc,
        a_sc,
        at_sc,
        x_sc,
        v_sc,
        e_sc,
        s_sc,
        part_sc,
        recv_sc,
        stage_sc,
        mask_sc,
        load_sem,
        wall_send,
        wall_recv,
        cell_send,
        cell_recv,
        ring_send,
        ring_recv,
        *step_sc,
    ) = refs
    loads = [
        pltpu.make_async_copy(operands[i], held[i], load_sem.at[i]) for i in range(OPERANDS)
    ]
    (
        cell_ref,
        shape_ref,
        harm_ref,
        centers_ref,
        force_ref,
        dest_ref,
        slot_ref,
        dest_s,
        slot_s,
        rank_s,
        couple_ref,
        pick_s,
        src_s,
        owner_s,
        srcb_ref,
        tgtb_ref,
        blocks_ref,
    ) = held
    for load in loads:
        load.start()
    clusters = centers_ref.shape[0]
    panels = centers_ref.shape[1] // 3
    near = dest_ref.shape[1]
    group = walls * clusters
    chunks = b_sc.shape[0]
    batch = LANES // (2 * ROWS)
    me_cell = lax.axis_index("cells")
    me = lax.axis_index("wall")

    def wall_peer(d):
        return lax.rem(me + d, walls)

    def cell_peer(d):
        return lax.rem(me_cell + d, cells)

    barrier = pltpu.get_barrier_semaphore()

    def greet_wall(i):
        pl.semaphore_signal(barrier, inc=1, device_id={"wall": wall_peer(i + 1)}, device_id_type=MESH)

    def greet_cell(i):
        pl.semaphore_signal(barrier, inc=1, device_id={"cells": cell_peer(i + 1)}, device_id_type=MESH)

    devices = cells * walls
    direct = devices <= 64

    def any_peer(d):
        peer = lax.rem(me_cell * walls + me + d, devices)
        return {"cells": lax.div(peer, walls), "wall": lax.rem(peer, walls)}

    def greet_any(i):
        pl.semaphore_signal(barrier, inc=1, device_id=any_peer(i + 1), device_id_type=MESH)

    if direct:
        each(devices - 1, greet_any)
    else:
        each(walls - 1, greet_wall)
        each(cells - 1, greet_cell)

    def column(row):
        size = row.shape[1]
        down = lax.broadcasted_iota(jnp.int32, (size, size), 0)
        across = lax.broadcasted_iota(jnp.int32, (size, size), 1)
        return jnp.sum(jnp.where(down == across, row, 0.0), axis=1, keepdims=True)

    a_sc[...] = jnp.zeros(a_sc.shape, BF16)
    for load in loads[:4]:
        load.wait()
    for s in range(clusters):
        x_sc[me * clusters + s] = centers_ref[s : s + 1, :]
    cell_col = column(cell_ref[...].astype(F32))
    cell_count = shape_ref.shape[2]
    lane_cell = lax.broadcasted_iota(jnp.int32, (near, cell_count), 1).astype(F32)
    onehot = (lane_cell == cell_col).astype(BF16)

    def pick(ref):
        return [
            lax.dot_general(onehot, ref[a], NT, preferred_element_type=F32).astype(BF16)
            for a in range(3)
        ]

    def put(row, half, value):
        for j in range(chunks):
            rows = pl.ds(half * ROWS + row, near, stride=2 * ROWS)
            b_sc[j, rows, :] = value[:, j * LANES : (j + 1) * LANES]

    picked = pick(shape_ref)

    pl.semaphore_wait(barrier, devices - 1 if direct else walls + cells - 2)

    def wall_copy(phase, d, src, dst):
        return pltpu.make_async_remote_copy(
            src_ref=src,
            dst_ref=dst,
            send_sem=wall_send.at[phase, d],
            recv_sem=wall_recv.at[phase, d],
            device_id={"wall": wall_peer(d)},
            device_id_type=MESH,
        )

    own = pl.ds(me * clusters, clusters)

    def center_copy(d):
        return wall_copy(0, d, x_sc.at[own], x_sc.at[own])

    each(walls - 1, lambda i: center_copy(i + 1).start())

    for load in loads[4:11]:
        load.wait()
    picked = jnp.concatenate(picked + pick(force_ref), axis=0)
    grid = rounded(jnp.dot(picked, harm_ref[...], preferred_element_type=F32))
    points = [grid[a * near : (a + 1) * near] for a in range(3)]
    forces = [grid[a * near : (a + 1) * near] for a in range(3, 6)]
    zero = jnp.zeros_like(points[0])
    one = zero + 1.0
    square = points[0] * points[0] + points[1] * points[1] + points[2] * points[2] + soft_core
    inner = points[0] * forces[0] + points[1] * forces[1] + points[2] * forces[2]
    for a in range(3):
        double = points[a] * -2.0
        for half, value in ((0, double), (1, forces[a])):
            put(a, half, value)
            put(12 + a, half, value)
        put(8 + a, 0, points[a])
        put(8 + a, 1, zero)
        put(3 + a, 0, one)
        put(3 + a, 1, zero)
    for row, sq, inn in zip((6, 7, 15), split3(square), split3(inner)):
        put(row, 0, sq)
        put(row, 1, -inn)
    put(11, 0, zero)
    put(11, 1, zero)

    def turn(g, carry):
        for j in range(chunks):
            width = min(LANES, points_count - j * LANES)
            tile = b_sc[j, pl.ds(pl.multiple_of(g * LANES, LANES), LANES), :]
            turned = jnp.transpose(tile.astype(BF16))
            bt_sc[g, j * LANES : j * LANES + width, :] = turned[:width]
        return carry

    lax.fori_loop(0, near // batch, turn, 0)

    rank_size = couple_ref.shape[2]
    far_blocks = couple_ref.shape[1]
    level_i = lax.broadcasted_iota(jnp.int32, (rank_size, rank_size), 0)
    level_j = lax.broadcasted_iota(jnp.int32, (rank_size, rank_size), 1)
    level = jnp.maximum(level_i, level_j)
    for t in range(clusters):
        for b in range(far_blocks):
            mask_sc[t, b] = jnp.where(level < rank_s[t, b], couple_ref[t, b], 0.0)

    flat = near * 8
    target_row = (dest_ref[...] * clusters + slot_ref[...]).astype(F32)
    spread = (
        lax.shift_right_logical(lax.broadcasted_iota(jnp.int32, (near, flat), 1), 3)
        == lax.broadcasted_iota(jnp.int32, (near, flat), 0)
    ).astype(F32)
    target_flat = jnp.dot(
        jnp.broadcast_to(target_row, (8, near)), spread, precision=HIGHEST, preferred_element_type=F32
    )[0:1]
    down = lax.broadcasted_iota(jnp.int32, (group * 8, flat), 0)
    across = lax.broadcasted_iota(jnp.int32, (group * 8, flat), 1)
    same = lax.shift_right_logical(down, 3).astype(F32) == target_flat
    e_sc[...] = jnp.where(same & ((down & 7) == (across & 7)), 1.0, 0.0).astype(BF16)

    kind = lax.broadcasted_iota(jnp.int32, (group, ROWS, panels), 1)
    at_sc[...] = jnp.where((kind == 6) | (kind == 7) | (kind == 15), 1.0, 0.0)
    each(walls - 1, lambda i: center_copy(i + 1).wait())

    def make_panels(t):
        for a in range(3):
            spot = x_sc[t][:, a * panels : (a + 1) * panels]
            first = rounded(spot)
            second = rounded(spot - first)
            whole = first + second
            at_sc[t, a : a + 1, :] = first
            at_sc[t, 12 + a : 13 + a, :] = second
            norm = whole * whole if a == 0 else norm + whole * whole
        for a, value in enumerate(split3(norm)):
            at_sc[t, 3 + a : 4 + a, :] = value
        rows = at_sc[t].astype(BF16)
        a_sc[t, 0:ROWS, 0:panels] = rows
        a_sc[t, ROWS : 2 * ROWS, panels : 2 * panels] = rows

    each(group, make_panels)

    empty = jnp.zeros((2 * ROWS, 2 * panels), BF16)

    def pair_rows(g, carry):
        for i in range(batch):
            r = g * batch + i
            panel = a_sc[dest_s[r] * clusters + slot_s[r]]
            weights = jnp.concatenate([panel if k == i else empty for k in range(batch)], axis=0)
            at = pl.ds(pl.multiple_of(r * 2 * ROWS, 2 * ROWS), 2 * ROWS)
            rows = jnp.concatenate([b_sc[j, at, :] for j in range(chunks)], axis=1).astype(BF16)
            total = jnp.zeros((2 * ROWS, 2 * panels), F32)
            whole = jnp.dot(bt_sc[g], weights, preferred_element_type=F32)
            for start in range(0, points_count, SPAN):
                stop = min(start + SPAN, points_count)
                both = whole[start:stop]
                inverse = lax.rsqrt(both[:, :panels])
                along = both[:, panels:] * (inverse * inverse * inverse)
                pair = jnp.concatenate([along.astype(BF16), inverse.astype(BF16)], axis=1)
                total += jnp.dot(rows[:, start:stop], pair, preferred_element_type=F32)
            summed = total[:ROWS, :panels] + total[ROWS:, panels:]
            v_sc[pl.ds(pl.multiple_of(r * 8, 8), 8), :] = summed[:8] + summed[8:]
        return carry

    lax.fori_loop(0, near // batch, pair_rows, 0)

    value = v_sc[...]
    high = value.astype(BF16)
    low_part = (value - high.astype(F32)).astype(BF16)
    select = e_sc[...]
    s_sc[...] = (
        jnp.dot(select, high, preferred_element_type=F32)
        + jnp.dot(select, low_part, preferred_element_type=F32)
    ).reshape(group, 8, panels)

    def make_part(t):
        for a in range(3):
            lanes = slice(a * panels, (a + 1) * panels)
            part_sc[t, :, lanes] = -stokes_scale * (
                s_sc[t, a : a + 1, :] + x_sc[t, :, lanes] * s_sc[t, 3:4, :]
            )

    each(group, make_part)

    def part_copy(d):
        return wall_copy(
            1, d, part_sc.at[pl.ds(wall_peer(d) * clusters, clusters)], recv_sc.at[me]
        )

    each(walls - 1, lambda i: part_copy(i + 1).start())
    recv_sc[me] = part_sc[own]
    each(walls - 1, lambda i: part_copy(i + 1).wait())
    total = jnp.sum(recv_sc[...], axis=0)
    rhs = [total[t] for t in range(clusters)]

    flat_i = lax.broadcasted_iota(jnp.int32, (rank_size, LANES), 0)
    flat_j = lax.broadcasted_iota(jnp.int32, (rank_size, LANES), 1)
    diagonal = flat_i == flat_j
    first_row = me_cell * group

    def apply_block(t, b, vector):
        low = jnp.broadcast_to(vector.astype(BF16), (ROWS, vector.shape[1]))
        return lax.dot_general(low, blocks_ref[t, b], NT, preferred_element_type=F32)[0:1]

    for load in loads[11:]:
        load.wait()
    density = rhs
    for step in range(ITERS):
        table_sc, nbr_sc = step_sc[2 * step : 2 * step + 2]
        ring = pltpu.make_async_remote_copy(
            src_ref=stage_sc.at[step],
            dst_ref=nbr_sc,
            send_sem=ring_send.at[step],
            recv_sem=ring_recv.at[step],
            device_id={"wall": wall_peer(1)},
            device_id_type=MESH,
        )
        for t in range(clusters):
            coef = jnp.sum(srcb_ref[t] * density[t], axis=1, keepdims=True)
            table_sc[first_row + me * clusters + t] = jnp.sum(
                jnp.where(diagonal, coef, 0.0), axis=0, keepdims=True
            )
            stage_sc[step, t] = density[t]
        mine = table_sc.at[pl.ds(first_row + me * clusters, clusters)]

        def coef_copy(d):
            return wall_copy(2 + step, d, mine, mine)

        def any_copy(d, rows):
            return pltpu.make_async_remote_copy(
                src_ref=rows,
                dst_ref=rows,
                send_sem=cell_send.at[step, 0],
                recv_sem=cell_recv.at[step, 0],
                device_id=any_peer(d),
                device_id_type=MESH,
            )

        block = table_sc.at[pl.ds(first_row, group)]

        def block_copy(d):
            return pltpu.make_async_remote_copy(
                src_ref=block,
                dst_ref=block,
                send_sem=cell_send.at[step, d],
                recv_sem=cell_recv.at[step, d],
                device_id={"cells": cell_peer(d)},
                device_id_type=MESH,
            )

        ring.start()
        if direct:
            each(devices - 1, lambda i: any_copy(i + 1, mine).start())
        else:
            each(walls - 1, lambda i: coef_copy(i + 1).start())
        near_term = [apply_block(t, 0, density[t]) for t in range(clusters)]
        if not direct:
            each(walls - 1, lambda i: coef_copy(i + 1).wait())
            each(cells - 1, lambda i: block_copy(i + 1).start())
        ring.wait()
        near_term = [
            near_term[t] + apply_block(t, 1, nbr_sc[pick_s[t]]) for t in range(clusters)
        ]
        if direct:
            any_copy(1, table_sc.at[pl.ds(0, (devices - 1) * clusters)]).wait()
        else:
            each(cells - 1, lambda i: block_copy(i + 1).wait())
        fresh = []
        for t in range(clusters):
            mixed = jnp.zeros((rank_size, rank_size), F32)
            for b in range(far_blocks):
                row = table_sc[owner_s[src_s[t, b]]]
                mixed += mask_sc[t, b] * row[:, :rank_size]
            mixed = jnp.sum(mixed, axis=1, keepdims=True)
            far_term = jnp.sum(tgtb_ref[t] * mixed, axis=0, keepdims=True)
            fresh.append(rhs[t] - near_term[t] - far_term)
        density = fresh
    for t in range(clusters):
        out_ref[t : t + 1, :] = density[t]


def local(
    shape_coef,
    force_coef,
    near_cell,
    near_dest,
    near_slot,
    panel_centers,
    near_blocks,
    near_pick,
    src_basis,
    far_couple,
    far_src,
    far_rank,
    tgt_basis,
    cluster_slot,
):
    cells = lax.axis_size("cells")
    walls = lax.axis_size("wall")
    near = near_cell.shape[0]
    clusters, width = panel_centers.shape
    panels = width // 3
    group = walls * clusters
    harmonic_host = harmonics(ORDER)
    harmonic = jnp.asarray(harmonic_host, F32).astype(BF16)
    grid_points = harmonic_host.shape[0]
    padded = -(-grid_points // LANES) * LANES
    harmonic_t = jnp.asarray(
        np.pad(harmonic_host.T, ((0, 0), (0, padded - grid_points))), F32
    ).astype(BF16)
    surface = jnp.einsum(
        "qs,asc->aqc", harmonic, shape_coef, preferred_element_type=F32
    ).astype(BF16)
    points_count = -(-grid_points // 16) * 16
    operands = (
        near_cell[None, :],
        shape_coef,
        harmonic_t,
        panel_centers,
        force_coef,
        near_dest[None, :],
        near_slot[None, :],
        near_dest,
        near_slot,
        far_rank,
        far_couple,
        near_pick,
        far_src,
        cluster_slot,
        jnp.transpose(src_basis, (0, 2, 1)),
        tgt_basis,
        near_blocks,
    )
    scalars = (7, 8, 9, 11, 12, 13)
    density = pl.pallas_call(
        functools.partial(wall_kernel, cells, walls, points_count),
        out_shape=jax.ShapeDtypeStruct((clusters, width), F32),
        in_specs=[pl.BlockSpec(memory_space=pltpu.HBM)] * OPERANDS,
        out_specs=pl.BlockSpec(memory_space=pltpu.VMEM),
        scratch_shapes=[
            (pltpu.SMEM if i in scalars else pltpu.VMEM)(array.shape, array.dtype)
            for i, array in enumerate(operands)
        ]
        + [
            pltpu.VMEM((padded // LANES, near * 2 * ROWS, LANES), F32),
            pltpu.VMEM((near * 2 * ROWS // LANES, points_count, LANES), BF16),
            pltpu.VMEM((group, 2 * ROWS, 2 * panels), BF16),
            pltpu.VMEM((group, ROWS, panels), F32),
            pltpu.VMEM((group, 1, width), F32),
            pltpu.VMEM((near * 8, panels), F32),
            pltpu.VMEM((group * 8, near * 8), BF16),
            pltpu.VMEM((group, 8, panels), F32),
            pltpu.VMEM((group, 1, width), F32),
            pltpu.VMEM((walls, clusters, 1, width), F32),
            pltpu.VMEM((ITERS, clusters, 1, width), F32),
            pltpu.VMEM(far_couple.shape, F32),
            pltpu.SemaphoreType.DMA((OPERANDS,)),
            pltpu.SemaphoreType.DMA((2 + ITERS, walls)),
            pltpu.SemaphoreType.DMA((2 + ITERS, walls)),
            pltpu.SemaphoreType.DMA((ITERS, cells)),
            pltpu.SemaphoreType.DMA((ITERS, cells)),
            pltpu.SemaphoreType.DMA((ITERS,)),
            pltpu.SemaphoreType.DMA((ITERS,)),
        ]
        + [
            pltpu.VMEM((cells * group, 1, LANES), F32),
            pltpu.VMEM((clusters, 1, width), F32),
        ]
        * ITERS,
        compiler_params=pltpu.CompilerParams(
            collective_id=0, has_side_effects=True, vmem_limit_bytes=60 * 1024 * 1024
        ),
    )(*operands)
    return (surface, density)


def solution(mesh):
    return jax.shard_map(
        local,
        mesh=mesh,
        in_specs=(
            P(None, None, ("cells", "wall")),
            P(None, None, ("cells", "wall")),
            P(("cells", "wall")),
            P(("cells", "wall")),
            P(("cells", "wall")),
            P(("cells", "wall"), None),
            P(("cells", "wall"), None, None, None),
            P(("cells", "wall")),
            P(("cells", "wall"), None, None),
            P(("cells", "wall"), None, None, None),
            P(("cells", "wall"), None),
            P(("cells", "wall"), None),
            P(("cells", "wall"), None, None),
            P(),
        ),
        out_specs=(P(None, None, ("cells", "wall")), P(("cells", "wall"), None)),
        check_vma=False,
    )
```

```python
import functools
import math

import jax
import jax.numpy as jnp
import numpy as np
from jax import lax
from jax.experimental import pallas as pl
from jax.experimental.pallas import tpu as pltpu
from jax.sharding import PartitionSpec as P

ORDER = 16
ITERS = 2
LANES = 128
ROWS = 16
SPAN = 256
OPERANDS = 17

soft_core = 0.25
stokes_scale = 1.0 / (8.0 * math.pi)

MESH = pl.DeviceIdType.MESH
HIGHEST = lax.Precision.HIGHEST
F32 = jnp.float32
BF16 = jnp.bfloat16
NT = (((1,), (1,)), ((), ()))


def harmonics(order):
    lat_count = order + 1
    polar_angle = np.pi * (np.arange(lat_count) + 0.5) / lat_count
    azimuth = np.pi * np.arange(2 * lat_count) / lat_count
    cos_polar = np.repeat(np.cos(polar_angle), 2 * lat_count)
    sin_polar = np.repeat(np.sin(polar_angle), 2 * lat_count)
    az_grid = np.tile(azimuth, lat_count)
    legendre = {}
    legendre[0, 0] = cos_polar * 0.0 + 0.5 / np.sqrt(np.pi)
    for m in range(1, order + 1):
        legendre[m, m] = -np.sqrt((2.0 * m + 1.0) / (2.0 * m)) * sin_polar * legendre[m - 1, m - 1]
    for m in range(order):
        legendre[m + 1, m] = np.sqrt(2.0 * m + 3.0) * cos_polar * legendre[m, m]
    for m in range(order + 1):
        for l in range(m + 2, order + 1):
            factor = np.sqrt((4.0 * l * l - 1.0) / (l * l - m * m))
            backward = np.sqrt(((l - 1.0) ** 2 - m * m) / (4.0 * (l - 1.0) ** 2 - 1.0))
            legendre[l, m] = factor * (
                cos_polar * legendre[l - 1, m] - backward * legendre[l - 2, m]
            )
    columns = []
    for l in range(order + 1):
        for m in range(-l, l + 1):
            if m > 0:
                columns.append(np.sqrt(2.0) * legendre[l, m] * np.cos(m * az_grid))
            elif m < 0:
                columns.append(np.sqrt(2.0) * legendre[l, -m] * np.sin(-m * az_grid))
            else:
                columns.append(legendre[l, 0])
    return np.stack(columns, axis=1)


def each(count, body):
    if count <= 32:
        for i in range(count):
            body(i)
    else:
        def step(i, carry):
            body(i)
            return carry

        lax.fori_loop(0, count, step, 0)


def rounded(value):
    return value.astype(BF16).astype(F32)


def split3(value):
    first = rounded(value)
    rest = value - first
    second = rounded(rest)
    return first, second, rounded(rest - second)


def wall_kernel(
    cells,
    walls,
    points_count,
    *refs,
):
    operands, refs = refs[:OPERANDS], refs[OPERANDS:]
    out_ref, refs = refs[0], refs[1:]
    held, refs = refs[:OPERANDS], refs[OPERANDS:]
    (
        b_sc,
        bt_sc,
        a_sc,
        at_sc,
        x_sc,
        v_sc,
        e_sc,
        s_sc,
        part_sc,
        recv_sc,
        stage_sc,
        mask_sc,
        load_sem,
        wall_send,
        wall_recv,
        cell_send,
        cell_recv,
        ring_send,
        ring_recv,
        *step_sc,
    ) = refs
    loads = [
        pltpu.make_async_copy(operands[i], held[i], load_sem.at[i]) for i in range(OPERANDS)
    ]
    (
        cell_ref,
        shape_ref,
        harm_ref,
        centers_ref,
        force_ref,
        dest_ref,
        slot_ref,
        dest_s,
        slot_s,
        rank_s,
        couple_ref,
        pick_s,
        src_s,
        owner_s,
        srcb_ref,
        tgtb_ref,
        blocks_ref,
    ) = held
    for load in loads:
        load.start()
    clusters = centers_ref.shape[0]
    panels = centers_ref.shape[1] // 3
    near = dest_ref.shape[1]
    group = walls * clusters
    padded = b_sc.shape[2]
    chunks = padded // LANES
    batch = LANES // (2 * ROWS)
    me_cell = lax.axis_index("cells")
    me = lax.axis_index("wall")

    def wall_peer(d):
        return lax.rem(me + d, walls)

    def cell_peer(d):
        return lax.rem(me_cell + d, cells)

    barrier = pltpu.get_barrier_semaphore()

    def greet_wall(i):
        pl.semaphore_signal(barrier, inc=1, device_id={"wall": wall_peer(i + 1)}, device_id_type=MESH)

    def greet_cell(i):
        pl.semaphore_signal(barrier, inc=1, device_id={"cells": cell_peer(i + 1)}, device_id_type=MESH)

    devices = cells * walls
    direct = devices <= 64

    def any_peer(d):
        peer = lax.rem(me_cell * walls + me + d, devices)
        return {"cells": lax.div(peer, walls), "wall": lax.rem(peer, walls)}

    def greet_any(i):
        pl.semaphore_signal(barrier, inc=1, device_id=any_peer(i + 1), device_id_type=MESH)

    if direct:
        each(devices - 1, greet_any)
    else:
        each(walls - 1, greet_wall)
        each(cells - 1, greet_cell)

    def column(row):
        size = row.shape[1]
        down = lax.broadcasted_iota(jnp.int32, (size, size), 0)
        across = lax.broadcasted_iota(jnp.int32, (size, size), 1)
        return jnp.sum(jnp.where(down == across, row, 0.0), axis=1, keepdims=True)

    a_sc[...] = jnp.zeros(a_sc.shape, BF16)
    for load in loads[:4]:
        load.wait()
    for s in range(clusters):
        x_sc[me * clusters + s] = centers_ref[s : s + 1, :]
    cell_col = column(cell_ref[...].astype(F32))
    cell_count = shape_ref.shape[2]
    lane_cell = lax.broadcasted_iota(jnp.int32, (near, cell_count), 1).astype(F32)
    onehot = (lane_cell == cell_col).astype(BF16)

    def pick(ref):
        return [
            lax.dot_general(onehot, ref[a], NT, preferred_element_type=F32).astype(BF16)
            for a in range(3)
        ]

    def put(row, half, value):
        b_sc[:, half * ROWS + row, :] = value

    picked = pick(shape_ref)

    pl.semaphore_wait(barrier, devices - 1 if direct else walls + cells - 2)

    def wall_copy(phase, d, src, dst):
        return pltpu.make_async_remote_copy(
            src_ref=src,
            dst_ref=dst,
            send_sem=wall_send.at[phase, d],
            recv_sem=wall_recv.at[phase, d],
            device_id={"wall": wall_peer(d)},
            device_id_type=MESH,
        )

    own = pl.ds(me * clusters, clusters)

    def center_copy(d):
        return wall_copy(0, d, x_sc.at[own], x_sc.at[own])

    each(walls - 1, lambda i: center_copy(i + 1).start())

    for load in loads[4:11]:
        load.wait()
    picked = jnp.concatenate(picked + pick(force_ref), axis=0)
    grid = rounded(jnp.dot(picked, harm_ref[...], preferred_element_type=F32))
    points = [grid[a * near : (a + 1) * near] for a in range(3)]
    forces = [grid[a * near : (a + 1) * near] for a in range(3, 6)]
    zero = jnp.zeros_like(points[0])
    one = zero + 1.0
    square = points[0] * points[0] + points[1] * points[1] + points[2] * points[2] + soft_core
    inner = points[0] * forces[0] + points[1] * forces[1] + points[2] * forces[2]
    for a in range(3):
        double = points[a] * -2.0
        for half, value in ((0, double), (1, forces[a])):
            put(a, half, value)
            put(12 + a, half, value)
        put(8 + a, 0, points[a])
        put(8 + a, 1, zero)
        put(3 + a, 0, one)
        put(3 + a, 1, zero)
    for row, sq, inn in zip((6, 7, 15), split3(square), split3(inner)):
        put(row, 0, sq)
        put(row, 1, -inn)
    put(11, 0, zero)
    put(11, 1, zero)

    def turn(g, carry):
        for j in range(chunks):
            width = min(LANES, points_count - j * LANES)
            tile = b_sc[pl.ds(g * batch, batch), :, j * LANES : (j + 1) * LANES]
            turned = jnp.transpose(tile.reshape(LANES, LANES).astype(BF16))
            bt_sc[g, j * LANES : j * LANES + width, :] = turned[:width]
        return carry

    lax.fori_loop(0, near // batch, turn, 0)

    rank_size = couple_ref.shape[2]
    far_blocks = couple_ref.shape[1]
    level_i = lax.broadcasted_iota(jnp.int32, (rank_size, rank_size), 0)
    level_j = lax.broadcasted_iota(jnp.int32, (rank_size, rank_size), 1)
    level = jnp.maximum(level_i, level_j)
    for t in range(clusters):
        for b in range(far_blocks):
            mask_sc[t, b] = jnp.where(level < rank_s[t, b], couple_ref[t, b], 0.0)

    flat = near * 8
    target_row = (dest_ref[...] * clusters + slot_ref[...]).astype(F32)
    spread = (
        lax.shift_right_logical(lax.broadcasted_iota(jnp.int32, (near, flat), 1), 3)
        == lax.broadcasted_iota(jnp.int32, (near, flat), 0)
    ).astype(F32)
    target_flat = jnp.dot(
        jnp.broadcast_to(target_row, (8, near)), spread, precision=HIGHEST, preferred_element_type=F32
    )[0:1]
    down = lax.broadcasted_iota(jnp.int32, (group * 8, flat), 0)
    across = lax.broadcasted_iota(jnp.int32, (group * 8, flat), 1)
    same = lax.shift_right_logical(down, 3).astype(F32) == target_flat
    e_sc[...] = jnp.where(same & ((down & 7) == (across & 7)), 1.0, 0.0).astype(BF16)

    kind = lax.broadcasted_iota(jnp.int32, (group, ROWS, panels), 1)
    at_sc[...] = jnp.where((kind == 6) | (kind == 7) | (kind == 15), 1.0, 0.0)
    each(walls - 1, lambda i: center_copy(i + 1).wait())

    def make_panels(t):
        for a in range(3):
            spot = x_sc[t][:, a * panels : (a + 1) * panels]
            first = rounded(spot)
            second = rounded(spot - first)
            whole = first + second
            at_sc[t, a : a + 1, :] = first
            at_sc[t, 12 + a : 13 + a, :] = second
            norm = whole * whole if a == 0 else norm + whole * whole
        for a, value in enumerate(split3(norm)):
            at_sc[t, 3 + a : 4 + a, :] = value
        rows = at_sc[t].astype(BF16)
        a_sc[t, 0:ROWS, 0:panels] = rows
        a_sc[t, ROWS : 2 * ROWS, panels : 2 * panels] = rows

    each(group, make_panels)

    empty = jnp.zeros((2 * ROWS, 2 * panels), BF16)

    def pair_rows(g, carry):
        for i in range(batch):
            r = g * batch + i
            panel = a_sc[dest_s[r] * clusters + slot_s[r]]
            weights = jnp.concatenate([panel if k == i else empty for k in range(batch)], axis=0)
            rows = b_sc[r].astype(BF16)
            total = jnp.zeros((2 * ROWS, 2 * panels), F32)
            whole = jnp.dot(bt_sc[g], weights, preferred_element_type=F32)
            for start in range(0, points_count, SPAN):
                stop = min(start + SPAN, points_count)
                both = whole[start:stop].astype(BF16)
                inverse = lax.rsqrt(both[:, :panels])
                along = both[:, panels:] * (inverse * inverse * inverse)
                pair = jnp.concatenate([along, inverse], axis=1)
                total += jnp.dot(rows[:, start:stop], pair, preferred_element_type=F32)
            summed = total[:ROWS, :panels] + total[ROWS:, panels:]
            v_sc[pl.ds(pl.multiple_of(r * 8, 8), 8), :] = summed[:8] + summed[8:]
        return carry

    lax.fori_loop(0, near // batch, pair_rows, 0)

    value = v_sc[...]
    high = value.astype(BF16)
    low_part = (value - high.astype(F32)).astype(BF16)
    select = e_sc[...]
    s_sc[...] = (
        jnp.dot(select, high, preferred_element_type=F32)
        + jnp.dot(select, low_part, preferred_element_type=F32)
    ).reshape(group, 8, panels)

    def make_part(t):
        for a in range(3):
            lanes = slice(a * panels, (a + 1) * panels)
            part_sc[t, :, lanes] = -stokes_scale * (
                s_sc[t, a : a + 1, :] + x_sc[t, :, lanes] * s_sc[t, 3:4, :]
            )

    each(group, make_part)

    def part_copy(d):
        return wall_copy(
            1, d, part_sc.at[pl.ds(wall_peer(d) * clusters, clusters)], recv_sc.at[me]
        )

    each(walls - 1, lambda i: part_copy(i + 1).start())
    recv_sc[me] = part_sc[own]
    each(walls - 1, lambda i: part_copy(i + 1).wait())
    total = jnp.sum(recv_sc[...], axis=0)
    rhs = [total[t] for t in range(clusters)]

    flat_i = lax.broadcasted_iota(jnp.int32, (rank_size, LANES), 0)
    flat_j = lax.broadcasted_iota(jnp.int32, (rank_size, LANES), 1)
    diagonal = flat_i == flat_j
    first_row = me_cell * group

    def apply_block(t, b, vector):
        low = jnp.broadcast_to(vector.astype(BF16), (ROWS, vector.shape[1]))
        return lax.dot_general(low, blocks_ref[t, b], NT, preferred_element_type=F32)[0:1]

    for load in loads[11:]:
        load.wait()
    density = rhs
    for step in range(ITERS):
        table_sc, nbr_sc = step_sc[2 * step : 2 * step + 2]
        ring = pltpu.make_async_remote_copy(
            src_ref=stage_sc.at[step],
            dst_ref=nbr_sc,
            send_sem=ring_send.at[step],
            recv_sem=ring_recv.at[step],
            device_id={"wall": wall_peer(1)},
            device_id_type=MESH,
        )
        for t in range(clusters):
            coef = jnp.sum(srcb_ref[t] * density[t], axis=1, keepdims=True)
            table_sc[first_row + me * clusters + t] = jnp.sum(
                jnp.where(diagonal, coef, 0.0), axis=0, keepdims=True
            )
            stage_sc[step, t] = density[t]
        mine = table_sc.at[pl.ds(first_row + me * clusters, clusters)]

        def coef_copy(d):
            return wall_copy(2 + step, d, mine, mine)

        def any_copy(d, rows):
            return pltpu.make_async_remote_copy(
                src_ref=rows,
                dst_ref=rows,
                send_sem=cell_send.at[step, 0],
                recv_sem=cell_recv.at[step, 0],
                device_id=any_peer(d),
                device_id_type=MESH,
            )

        block = table_sc.at[pl.ds(first_row, group)]

        def block_copy(d):
            return pltpu.make_async_remote_copy(
                src_ref=block,
                dst_ref=block,
                send_sem=cell_send.at[step, d],
                recv_sem=cell_recv.at[step, d],
                device_id={"cells": cell_peer(d)},
                device_id_type=MESH,
            )

        ring.start()
        if direct:
            each(devices - 1, lambda i: any_copy(i + 1, mine).start())
        else:
            each(walls - 1, lambda i: coef_copy(i + 1).start())
        near_term = [apply_block(t, 0, density[t]) for t in range(clusters)]
        if not direct:
            each(walls - 1, lambda i: coef_copy(i + 1).wait())
            each(cells - 1, lambda i: block_copy(i + 1).start())
        ring.wait()
        near_term = [
            near_term[t] + apply_block(t, 1, nbr_sc[pick_s[t]]) for t in range(clusters)
        ]
        if direct:
            any_copy(1, table_sc.at[pl.ds(0, (devices - 1) * clusters)]).wait()
        else:
            each(cells - 1, lambda i: block_copy(i + 1).wait())
        fresh = []
        for t in range(clusters):
            mixed = jnp.zeros((rank_size, rank_size), F32)
            for b in range(far_blocks):
                row = table_sc[owner_s[src_s[t, b]]]
                mixed += mask_sc[t, b] * row[:, :rank_size]
            mixed = jnp.sum(mixed, axis=1, keepdims=True)
            far_term = jnp.sum(tgtb_ref[t] * mixed, axis=0, keepdims=True)
            fresh.append(rhs[t] - near_term[t] - far_term)
        density = fresh
    for t in range(clusters):
        out_ref[t : t + 1, :] = density[t]


def local(
    shape_coef,
    force_coef,
    near_cell,
    near_dest,
    near_slot,
    panel_centers,
    near_blocks,
    near_pick,
    src_basis,
    far_couple,
    far_src,
    far_rank,
    tgt_basis,
    cluster_slot,
):
    cells = lax.axis_size("cells")
    walls = lax.axis_size("wall")
    near = near_cell.shape[0]
    clusters, width = panel_centers.shape
    panels = width // 3
    group = walls * clusters
    harmonic_host = harmonics(ORDER)
    harmonic = jnp.asarray(harmonic_host, F32).astype(BF16)
    grid_points = harmonic_host.shape[0]
    padded = -(-grid_points // LANES) * LANES
    harmonic_t = jnp.asarray(
        np.pad(harmonic_host.T, ((0, 0), (0, padded - grid_points))), F32
    ).astype(BF16)
    surface = jnp.einsum(
        "qs,asc->aqc", harmonic, shape_coef, preferred_element_type=F32
    ).astype(BF16)
    points_count = -(-grid_points // 16) * 16
    operands = (
        near_cell[None, :],
        shape_coef,
        harmonic_t,
        panel_centers,
        force_coef,
        near_dest[None, :],
        near_slot[None, :],
        near_dest,
        near_slot,
        far_rank,
        far_couple,
        near_pick,
        far_src,
        cluster_slot,
        jnp.transpose(src_basis, (0, 2, 1)),
        tgt_basis,
        near_blocks,
    )
    scalars = (7, 8, 9, 11, 12, 13)
    density = pl.pallas_call(
        functools.partial(wall_kernel, cells, walls, points_count),
        out_shape=jax.ShapeDtypeStruct((clusters, width), F32),
        in_specs=[pl.BlockSpec(memory_space=pltpu.HBM)] * OPERANDS,
        out_specs=pl.BlockSpec(memory_space=pltpu.VMEM),
        scratch_shapes=[
            (pltpu.SMEM if i in scalars else pltpu.VMEM)(array.shape, array.dtype)
            for i, array in enumerate(operands)
        ]
        + [
            pltpu.VMEM((near, 2 * ROWS, padded), F32),
            pltpu.VMEM((near * 2 * ROWS // LANES, points_count, LANES), BF16),
            pltpu.VMEM((group, 2 * ROWS, 2 * panels), BF16),
            pltpu.VMEM((group, ROWS, panels), F32),
            pltpu.VMEM((group, 1, width), F32),
            pltpu.VMEM((near * 8, panels), F32),
            pltpu.VMEM((group * 8, near * 8), BF16),
            pltpu.VMEM((group, 8, panels), F32),
            pltpu.VMEM((group, 1, width), F32),
            pltpu.VMEM((walls, clusters, 1, width), F32),
            pltpu.VMEM((ITERS, clusters, 1, width), F32),
            pltpu.VMEM(far_couple.shape, F32),
            pltpu.SemaphoreType.DMA((OPERANDS,)),
            pltpu.SemaphoreType.DMA((2 + ITERS, walls)),
            pltpu.SemaphoreType.DMA((2 + ITERS, walls)),
            pltpu.SemaphoreType.DMA((ITERS, cells)),
            pltpu.SemaphoreType.DMA((ITERS, cells)),
            pltpu.SemaphoreType.DMA((ITERS,)),
            pltpu.SemaphoreType.DMA((ITERS,)),
        ]
        + [
            pltpu.VMEM((cells * group, 1, LANES), F32),
            pltpu.VMEM((clusters, 1, width), F32),
        ]
        * ITERS,
        compiler_params=pltpu.CompilerParams(
            collective_id=0, has_side_effects=True, vmem_limit_bytes=60 * 1024 * 1024
        ),
    )(*operands)
    return (surface, density)


def solution(mesh):
    return jax.shard_map(
        local,
        mesh=mesh,
        in_specs=(
            P(None, None, ("cells", "wall")),
            P(None, None, ("cells", "wall")),
            P(("cells", "wall")),
            P(("cells", "wall")),
            P(("cells", "wall")),
            P(("cells", "wall"), None),
            P(("cells", "wall"), None, None, None),
            P(("cells", "wall")),
            P(("cells", "wall"), None, None),
            P(("cells", "wall"), None, None, None),
            P(("cells", "wall"), None),
            P(("cells", "wall"), None),
            P(("cells", "wall"), None, None),
            P(),
        ),
        out_specs=(P(None, None, ("cells", "wall")), P(("cells", "wall"), None)),
        check_vma=False,
    )
```

```python
import functools
import math

import jax
import jax.numpy as jnp
import numpy as np
from jax import lax
from jax.experimental import pallas as pl
from jax.experimental.pallas import tpu as pltpu
from jax.sharding import PartitionSpec as P

ORDER = 16
ITERS = 2
LANES = 128
ROWS = 16
SPAN = 256
OPERANDS = 17

soft_core = 0.25
stokes_scale = 1.0 / (8.0 * math.pi)

MESH = pl.DeviceIdType.MESH
HIGHEST = lax.Precision.HIGHEST
F32 = jnp.float32
BF16 = jnp.bfloat16
NT = (((1,), (1,)), ((), ()))


def harmonics(order):
    lat_count = order + 1
    polar_angle = np.pi * (np.arange(lat_count) + 0.5) / lat_count
    azimuth = np.pi * np.arange(2 * lat_count) / lat_count
    cos_polar = np.repeat(np.cos(polar_angle), 2 * lat_count)
    sin_polar = np.repeat(np.sin(polar_angle), 2 * lat_count)
    az_grid = np.tile(azimuth, lat_count)
    legendre = {}
    legendre[0, 0] = cos_polar * 0.0 + 0.5 / np.sqrt(np.pi)
    for m in range(1, order + 1):
        legendre[m, m] = -np.sqrt((2.0 * m + 1.0) / (2.0 * m)) * sin_polar * legendre[m - 1, m - 1]
    for m in range(order):
        legendre[m + 1, m] = np.sqrt(2.0 * m + 3.0) * cos_polar * legendre[m, m]
    for m in range(order + 1):
        for l in range(m + 2, order + 1):
            factor = np.sqrt((4.0 * l * l - 1.0) / (l * l - m * m))
            backward = np.sqrt(((l - 1.0) ** 2 - m * m) / (4.0 * (l - 1.0) ** 2 - 1.0))
            legendre[l, m] = factor * (
                cos_polar * legendre[l - 1, m] - backward * legendre[l - 2, m]
            )
    columns = []
    for l in range(order + 1):
        for m in range(-l, l + 1):
            if m > 0:
                columns.append(np.sqrt(2.0) * legendre[l, m] * np.cos(m * az_grid))
            elif m < 0:
                columns.append(np.sqrt(2.0) * legendre[l, -m] * np.sin(-m * az_grid))
            else:
                columns.append(legendre[l, 0])
    return np.stack(columns, axis=1)


def each(count, body):
    if count <= 32:
        for i in range(count):
            body(i)
    else:
        def step(i, carry):
            body(i)
            return carry

        lax.fori_loop(0, count, step, 0)


def rounded(value):
    return value.astype(BF16).astype(F32)


def split2(value):
    first = rounded(value)
    return first, rounded(value - first)


def split3(value):
    first = rounded(value)
    rest = value - first
    second = rounded(rest)
    return first, second, rounded(rest - second)


def wall_kernel(
    cells,
    walls,
    points_count,
    *refs,
):
    operands, refs = refs[:OPERANDS], refs[OPERANDS:]
    out_ref, refs = refs[0], refs[1:]
    held, refs = refs[:OPERANDS], refs[OPERANDS:]
    (
        b_sc,
        bt_sc,
        a_sc,
        at_sc,
        x_sc,
        v_sc,
        e_sc,
        s_sc,
        part_sc,
        recv_sc,
        stage_sc,
        mask_sc,
        load_sem,
        wall_send,
        wall_recv,
        cell_send,
        cell_recv,
        ring_send,
        ring_recv,
        *step_sc,
    ) = refs
    loads = [
        pltpu.make_async_copy(operands[i], held[i], load_sem.at[i]) for i in range(OPERANDS)
    ]
    (
        cell_ref,
        shape_ref,
        harm_ref,
        centers_ref,
        force_ref,
        dest_ref,
        slot_ref,
        dest_s,
        slot_s,
        rank_s,
        couple_ref,
        pick_s,
        src_s,
        owner_s,
        srcb_ref,
        tgtb_ref,
        blocks_ref,
    ) = held
    for load in loads:
        load.start()
    clusters = centers_ref.shape[0]
    panels = centers_ref.shape[1] // 3
    near = dest_ref.shape[1]
    group = walls * clusters
    padded = b_sc.shape[2]
    chunks = padded // LANES
    batch = LANES // (2 * ROWS)
    me_cell = lax.axis_index("cells")
    me = lax.axis_index("wall")

    def wall_peer(d):
        return lax.rem(me + d, walls)

    def cell_peer(d):
        return lax.rem(me_cell + d, cells)

    barrier = pltpu.get_barrier_semaphore()

    def greet_wall(i):
        pl.semaphore_signal(barrier, inc=1, device_id={"wall": wall_peer(i + 1)}, device_id_type=MESH)

    def greet_cell(i):
        pl.semaphore_signal(barrier, inc=1, device_id={"cells": cell_peer(i + 1)}, device_id_type=MESH)

    devices = cells * walls
    direct = devices <= 64

    def any_peer(d):
        peer = lax.rem(me_cell * walls + me + d, devices)
        return {"cells": lax.div(peer, walls), "wall": lax.rem(peer, walls)}

    def greet_any(i):
        pl.semaphore_signal(barrier, inc=1, device_id=any_peer(i + 1), device_id_type=MESH)

    if direct:
        each(devices - 1, greet_any)
    else:
        each(walls - 1, greet_wall)
        each(cells - 1, greet_cell)

    def column(row):
        size = row.shape[1]
        down = lax.broadcasted_iota(jnp.int32, (size, size), 0)
        across = lax.broadcasted_iota(jnp.int32, (size, size), 1)
        return jnp.sum(jnp.where(down == across, row, 0.0), axis=1, keepdims=True)

    a_sc[...] = jnp.zeros(a_sc.shape, BF16)
    for load in loads[:4]:
        load.wait()
    for s in range(clusters):
        x_sc[me * clusters + s] = centers_ref[s : s + 1, :]
    cell_col = column(cell_ref[...].astype(F32))
    cell_count = shape_ref.shape[2]
    lane_cell = lax.broadcasted_iota(jnp.int32, (near, cell_count), 1).astype(F32)
    onehot = (lane_cell == cell_col).astype(BF16)

    def pick(ref):
        return [
            lax.dot_general(onehot, ref[a], NT, preferred_element_type=F32).astype(BF16)
            for a in range(3)
        ]

    def put(row, half, value):
        b_sc[:, half * ROWS + row, :] = value

    picked = pick(shape_ref)

    pl.semaphore_wait(barrier, devices - 1 if direct else walls + cells - 2)

    def wall_copy(phase, d, src, dst):
        return pltpu.make_async_remote_copy(
            src_ref=src,
            dst_ref=dst,
            send_sem=wall_send.at[phase, d],
            recv_sem=wall_recv.at[phase, d],
            device_id={"wall": wall_peer(d)},
            device_id_type=MESH,
        )

    own = pl.ds(me * clusters, clusters)

    def center_copy(d):
        return wall_copy(0, d, x_sc.at[own], x_sc.at[own])

    each(walls - 1, lambda i: center_copy(i + 1).start())

    for load in loads[4:11]:
        load.wait()
    picked = jnp.concatenate(picked + pick(force_ref), axis=0)
    grid = rounded(jnp.dot(picked, harm_ref[...], preferred_element_type=F32))
    points = [grid[a * near : (a + 1) * near] for a in range(3)]
    forces = [grid[a * near : (a + 1) * near] for a in range(3, 6)]
    part = lax.broadcasted_iota(jnp.int32, b_sc.shape[1:], 0)
    fixed = jnp.where((part >= 3) & (part < 6), 1.0, 0.0)

    def fill(r, carry):
        b_sc[r] = fixed
        return carry

    lax.fori_loop(0, near, fill, 0, unroll=4)
    square = points[0] * points[0] + points[1] * points[1] + points[2] * points[2] + soft_core
    inner = points[0] * forces[0] + points[1] * forces[1] + points[2] * forces[2]
    for a in range(3):
        double = points[a] * -2.0
        for half, value in ((0, double), (1, forces[a])):
            put(a, half, value)
            put(12 + a, half, value)
        put(8 + a, 0, points[a])
    for row, sq, inn in zip((6, 7), split2(square), split2(inner)):
        put(row, 0, sq)
        put(row, 1, -inn)

    def turn(g, carry):
        for j in range(chunks):
            width = min(LANES, points_count - j * LANES)
            tile = b_sc[pl.ds(g * batch, batch), :, j * LANES : (j + 1) * LANES]
            turned = jnp.transpose(tile.reshape(LANES, LANES).astype(BF16))
            bt_sc[g, j * LANES : j * LANES + width, :] = turned[:width]
        return carry

    lax.fori_loop(0, near // batch, turn, 0)

    rank_size = couple_ref.shape[2]
    far_blocks = couple_ref.shape[1]
    level_i = lax.broadcasted_iota(jnp.int32, (rank_size, rank_size), 0)
    level_j = lax.broadcasted_iota(jnp.int32, (rank_size, rank_size), 1)
    level = jnp.maximum(level_i, level_j)
    for t in range(clusters):
        for b in range(far_blocks):
            mask_sc[t, b] = jnp.where(level < rank_s[t, b], couple_ref[t, b], 0.0)

    flat = near * 8
    target_row = (dest_ref[...] * clusters + slot_ref[...]).astype(F32)
    spread = (
        lax.shift_right_logical(lax.broadcasted_iota(jnp.int32, (near, flat), 1), 3)
        == lax.broadcasted_iota(jnp.int32, (near, flat), 0)
    ).astype(F32)
    target_flat = jnp.dot(
        jnp.broadcast_to(target_row, (8, near)), spread, precision=HIGHEST, preferred_element_type=F32
    )[0:1]
    down = lax.broadcasted_iota(jnp.int32, (group * 8, flat), 0)
    across = lax.broadcasted_iota(jnp.int32, (group * 8, flat), 1)
    same = lax.shift_right_logical(down, 3).astype(F32) == target_flat
    e_sc[...] = jnp.where(same & ((down & 7) == (across & 7)), 1.0, 0.0).astype(BF16)

    kind = lax.broadcasted_iota(jnp.int32, (group, ROWS, panels), 1)
    at_sc[...] = jnp.where((kind == 6) | (kind == 7) | (kind == 15), 1.0, 0.0)
    each(walls - 1, lambda i: center_copy(i + 1).wait())

    def make_panels(t):
        for a in range(3):
            spot = x_sc[t][:, a * panels : (a + 1) * panels]
            first = rounded(spot)
            second = rounded(spot - first)
            whole = first + second
            at_sc[t, a : a + 1, :] = first
            at_sc[t, 12 + a : 13 + a, :] = second
            norm = whole * whole if a == 0 else norm + whole * whole
        for a, value in enumerate(split3(norm)):
            at_sc[t, 3 + a : 4 + a, :] = value
        rows = at_sc[t].astype(BF16)
        a_sc[t, 0:ROWS, 0:panels] = rows
        a_sc[t, ROWS : 2 * ROWS, panels : 2 * panels] = rows

    each(group, make_panels)

    empty = jnp.zeros((2 * ROWS, 2 * panels), BF16)

    def fields(g, i):
        r = g * batch + i
        panel = a_sc[dest_s[r] * clusters + slot_s[r]]
        weights = jnp.concatenate([panel if k == i else empty for k in range(batch)], axis=0)
        return jnp.dot(bt_sc[g], weights, preferred_element_type=F32)

    def reduce_row(r, whole):
        rows = b_sc[r].astype(BF16)
        total = jnp.zeros((2 * ROWS, 2 * panels), F32)
        for start in range(0, points_count, SPAN):
            stop = min(start + SPAN, points_count)
            both = whole[start:stop]
            inverse = lax.rsqrt(both[:, :panels])
            along = both[:, panels:] * (inverse * inverse * inverse)
            pair = jnp.concatenate([along.astype(BF16), inverse.astype(BF16)], axis=1)
            total += jnp.dot(rows[:, start:stop], pair, preferred_element_type=F32)
        summed = total[:ROWS, :panels] + total[ROWS:, panels:]
        v_sc[pl.ds(pl.multiple_of(r * 8, 8), 8), :] = summed[:8] + summed[8:]

    joined = math.gcd(near // batch, 2)

    def pair_rows(n, carry):
        places = [(n * joined + k, i) for k in range(joined) for i in range(batch)]
        ahead = fields(*places[0])
        for at, (g, i) in enumerate(places):
            whole = ahead
            if at + 1 < len(places):
                ahead = fields(*places[at + 1])
            reduce_row(g * batch + i, whole)
        return carry

    lax.fori_loop(0, near // batch // joined, pair_rows, 0)

    value = v_sc[...]
    high = value.astype(BF16)
    low_part = (value - high.astype(F32)).astype(BF16)
    select = e_sc[...]
    s_sc[...] = (
        jnp.dot(select, high, preferred_element_type=F32)
        + jnp.dot(select, low_part, preferred_element_type=F32)
    ).reshape(group, 8, panels)

    def make_part(t):
        for a in range(3):
            lanes = slice(a * panels, (a + 1) * panels)
            part_sc[t, :, lanes] = -stokes_scale * (
                s_sc[t, a : a + 1, :] + x_sc[t, :, lanes] * s_sc[t, 3:4, :]
            )

    each(group, make_part)

    def part_copy(d):
        return wall_copy(
            1, d, part_sc.at[pl.ds(wall_peer(d) * clusters, clusters)], recv_sc.at[me]
        )

    each(walls - 1, lambda i: part_copy(i + 1).start())
    recv_sc[me] = part_sc[own]
    each(walls - 1, lambda i: part_copy(i + 1).wait())
    total = jnp.sum(recv_sc[...], axis=0)
    rhs = [total[t] for t in range(clusters)]

    flat_i = lax.broadcasted_iota(jnp.int32, (rank_size, LANES), 0)
    flat_j = lax.broadcasted_iota(jnp.int32, (rank_size, LANES), 1)
    diagonal = flat_i == flat_j
    first_row = me_cell * group

    def apply_block(t, b, vector):
        low = jnp.broadcast_to(vector.astype(BF16), (ROWS, vector.shape[1]))
        return lax.dot_general(low, blocks_ref[t, b], NT, preferred_element_type=F32)[0:1]

    for load in loads[11:]:
        load.wait()
    density = rhs
    for step in range(ITERS):
        table_sc, nbr_sc = step_sc[2 * step : 2 * step + 2]
        ring = pltpu.make_async_remote_copy(
            src_ref=stage_sc.at[step],
            dst_ref=nbr_sc,
            send_sem=ring_send.at[step],
            recv_sem=ring_recv.at[step],
            device_id={"wall": wall_peer(1)},
            device_id_type=MESH,
        )
        for t in range(clusters):
            coef = jnp.sum(srcb_ref[t] * density[t], axis=1, keepdims=True)
            table_sc[first_row + me * clusters + t] = jnp.sum(
                jnp.where(diagonal, coef, 0.0), axis=0, keepdims=True
            )
            stage_sc[step, t] = density[t]
        mine = table_sc.at[pl.ds(first_row + me * clusters, clusters)]

        def coef_copy(d):
            return wall_copy(2 + step, d, mine, mine)

        def any_copy(d, rows):
            return pltpu.make_async_remote_copy(
                src_ref=rows,
                dst_ref=rows,
                send_sem=cell_send.at[step, 0],
                recv_sem=cell_recv.at[step, 0],
                device_id=any_peer(d),
                device_id_type=MESH,
            )

        block = table_sc.at[pl.ds(first_row, group)]

        def block_copy(d):
            return pltpu.make_async_remote_copy(
                src_ref=block,
                dst_ref=block,
                send_sem=cell_send.at[step, d],
                recv_sem=cell_recv.at[step, d],
                device_id={"cells": cell_peer(d)},
                device_id_type=MESH,
            )

        ring.start()
        if direct:
            each(devices - 1, lambda i: any_copy(i + 1, mine).start())
        else:
            each(walls - 1, lambda i: coef_copy(i + 1).start())
        near_term = [apply_block(t, 0, density[t]) for t in range(clusters)]
        if not direct:
            each(walls - 1, lambda i: coef_copy(i + 1).wait())
            each(cells - 1, lambda i: block_copy(i + 1).start())
        ring.wait()
        near_term = [
            near_term[t] + apply_block(t, 1, nbr_sc[pick_s[t]]) for t in range(clusters)
        ]
        if direct:
            any_copy(1, table_sc.at[pl.ds(0, (devices - 1) * clusters)]).wait()
        else:
            each(cells - 1, lambda i: block_copy(i + 1).wait())
        fresh = []
        for t in range(clusters):
            mixed = jnp.zeros((rank_size, rank_size), F32)
            for b in range(far_blocks):
                row = table_sc[owner_s[src_s[t, b]]]
                mixed += mask_sc[t, b] * row[:, :rank_size]
            mixed = jnp.sum(mixed, axis=1, keepdims=True)
            far_term = jnp.sum(tgtb_ref[t] * mixed, axis=0, keepdims=True)
            fresh.append(rhs[t] - near_term[t] - far_term)
        density = fresh
    for t in range(clusters):
        out_ref[t : t + 1, :] = density[t]


def local(
    shape_coef,
    force_coef,
    near_cell,
    near_dest,
    near_slot,
    panel_centers,
    near_blocks,
    near_pick,
    src_basis,
    far_couple,
    far_src,
    far_rank,
    tgt_basis,
    cluster_slot,
):
    cells = lax.axis_size("cells")
    walls = lax.axis_size("wall")
    near = near_cell.shape[0]
    clusters, width = panel_centers.shape
    panels = width // 3
    group = walls * clusters
    harmonic_host = harmonics(ORDER)
    harmonic = jnp.asarray(harmonic_host, F32).astype(BF16)
    grid_points = harmonic_host.shape[0]
    padded = -(-grid_points // LANES) * LANES
    harmonic_t = jnp.asarray(
        np.pad(harmonic_host.T, ((0, 0), (0, padded - grid_points))), F32
    ).astype(BF16)
    surface = jnp.einsum(
        "qs,asc->aqc", harmonic, shape_coef, preferred_element_type=F32
    ).astype(BF16)
    points_count = -(-grid_points // 16) * 16
    operands = (
        near_cell[None, :],
        shape_coef,
        harmonic_t,
        panel_centers,
        force_coef,
        near_dest[None, :],
        near_slot[None, :],
        near_dest,
        near_slot,
        far_rank,
        far_couple,
        near_pick,
        far_src,
        cluster_slot,
        jnp.transpose(src_basis, (0, 2, 1)),
        tgt_basis,
        near_blocks,
    )
    scalars = (7, 8, 9, 11, 12, 13)
    density = pl.pallas_call(
        functools.partial(wall_kernel, cells, walls, points_count),
        out_shape=jax.ShapeDtypeStruct((clusters, width), F32),
        in_specs=[pl.BlockSpec(memory_space=pltpu.HBM)] * OPERANDS,
        out_specs=pl.BlockSpec(memory_space=pltpu.VMEM),
        scratch_shapes=[
            (pltpu.SMEM if i in scalars else pltpu.VMEM)(array.shape, array.dtype)
            for i, array in enumerate(operands)
        ]
        + [
            pltpu.VMEM((near, 2 * ROWS, padded), F32),
            pltpu.VMEM((near * 2 * ROWS // LANES, points_count, LANES), BF16),
            pltpu.VMEM((group, 2 * ROWS, 2 * panels), BF16),
            pltpu.VMEM((group, ROWS, panels), F32),
            pltpu.VMEM((group, 1, width), F32),
            pltpu.VMEM((near * 8, panels), F32),
            pltpu.VMEM((group * 8, near * 8), BF16),
            pltpu.VMEM((group, 8, panels), F32),
            pltpu.VMEM((group, 1, width), F32),
            pltpu.VMEM((walls, clusters, 1, width), F32),
            pltpu.VMEM((ITERS, clusters, 1, width), F32),
            pltpu.VMEM(far_couple.shape, F32),
            pltpu.SemaphoreType.DMA((OPERANDS,)),
            pltpu.SemaphoreType.DMA((2 + ITERS, walls)),
            pltpu.SemaphoreType.DMA((2 + ITERS, walls)),
            pltpu.SemaphoreType.DMA((ITERS, cells)),
            pltpu.SemaphoreType.DMA((ITERS, cells)),
            pltpu.SemaphoreType.DMA((ITERS,)),
            pltpu.SemaphoreType.DMA((ITERS,)),
        ]
        + [
            pltpu.VMEM((cells * group, 1, LANES), F32),
            pltpu.VMEM((clusters, 1, width), F32),
        ]
        * ITERS,
        compiler_params=pltpu.CompilerParams(
            collective_id=0, has_side_effects=True, vmem_limit_bytes=60 * 1024 * 1024
        ),
    )(*operands)
    return (surface, density)


def solution(mesh):
    return jax.shard_map(
        local,
        mesh=mesh,
        in_specs=(
            P(None, None, ("cells", "wall")),
            P(None, None, ("cells", "wall")),
            P(("cells", "wall")),
            P(("cells", "wall")),
            P(("cells", "wall")),
            P(("cells", "wall"), None),
            P(("cells", "wall"), None, None, None),
            P(("cells", "wall")),
            P(("cells", "wall"), None, None),
            P(("cells", "wall"), None, None, None),
            P(("cells", "wall"), None),
            P(("cells", "wall"), None),
            P(("cells", "wall"), None, None),
            P(),
        ),
        out_specs=(P(None, None, ("cells", "wall")), P(("cells", "wall"), None)),
        check_vma=False,
    )
```
